256 devices in a mesh: vel: 32 (over z, x), mesh: 8 (over y, core).
Axes of the slice: x: 4, y: 4, z: 8, core: 2. Of those that a mesh axis runs over, the one named last changes fastest.
Arguments:
- dist_old: float32 [256, 262144], P('mesh', 'vel'), may hold values from 0 to 9, as said below
- volume: float32 [256], P('mesh'), may hold values from 0.5 to 2
- area: float32 [4, 256], P(None, 'mesh'), may hold values from 0.3 to 1.5
- normals: float32 [3, 4, 256], P(None, None, 'mesh')
- neighbor: int32 [4, 256], P(None, 'mesh'), may hold values from 0 to 96, as said below
- union_rows: int32 [8, 16], P('mesh'), may hold values from 0 to 31
- union_index: int32 [8, 8, 8], replicated, may hold values from 0 to 15
Outputs:
- dist_new: float32 [256, 262144], P('mesh', 'vel')
- cell_moment_table: float32 [14, 256], P(None, 'mesh')
The draws below stay inside these ranges and needn't reach their ends.
Inputs may be any that keep to these rules, and one draw needn't show every extreme that they name: `dist_old`: every entry is nonnegative. `neighbor`: for a cell of partition p: values below 32 name a cell of p; 32 + s * 8 + t names slot t of what partition s sends to p, with s != p; 96 names the free stream.
All inputs are finite; a program needn't handle non-finite values.
Results may differ from the reference program's by a relative error of at most 0.0003.
Values sent between devices are 32-bit elements; how exact they have to be, the bound alone decides.
No kernel may reach another device: no remote copies, remote signals or barrier semaphores. Data moves between devices by JAX's collectives and lax.ppermute only.
A program may use at most 64 MiB of HBM per device.

```python
import math
import jax
import jax.numpy as jnp
from jax import lax

VGRID = 64
CELL_DEV = 32
CELLS = 256
FACES = 4
HALO = 8
UNION = 16
ITERS = 3
N_MESH = 8


def grid_coords_drawn(start, count):
    index = start + jnp.arange(count, dtype=jnp.int32)
    spacing = 20.0 / VGRID
    first = index // (VGRID * VGRID)
    second = index // VGRID % VGRID
    third = index % VGRID

    def place(level):
        return (level.astype(jnp.float32) + 0.5) * spacing - 10.0
    return (place(first), place(second), place(third))


def draw_dist_old(key, part):
    key = jax.random.fold_in(key, 17)
    seed_handles = jax.random.split(key, 6)
    overall_quantity = CELL_DEV * N_MESH
    speed_x, speed_y, speed_z = grid_coords_drawn(0, VGRID ** 3)
    local_concentration = jnp.exp(jax.random.uniform(seed_handles[0], (overall_quantity,), jnp.float32, math.log(0.5), math.log(2.0)))
    flow_x = jax.random.uniform(seed_handles[1], (overall_quantity,), jnp.float32, -5.0, 5.0)
    flow_y = jax.random.uniform(seed_handles[2], (overall_quantity,), jnp.float32, -5.0, 5.0)
    flow_z = jax.random.uniform(seed_handles[3], (overall_quantity,), jnp.float32, -5.0, 5.0)
    thermal_level = jax.random.uniform(seed_handles[4], (overall_quantity,), jnp.float32, 0.6, 2.5)
    rough = 0.4 * jax.random.uniform(seed_handles[5], (overall_quantity, VGRID ** 3), jnp.float32, -1.0, 1.0)
    peculiar_speed_norm = (speed_x[None, :] - flow_x[:, None]) ** 2 + (speed_y[None, :] - flow_y[:, None]) ** 2 + (speed_z[None, :] - flow_z[:, None]) ** 2
    equilibrium_distribution = (local_concentration * thermal_level ** (-1.5))[:, None] * jnp.exp(-peculiar_speed_norm / (2.0 * thermal_level[:, None]))
    return equilibrium_distribution * (1.0 + rough)


def draw_normals(key, part):
    key = jax.random.fold_in(key, 13)
    key_angle, key_height = jax.random.split(key)
    overall_quantity = CELL_DEV * N_MESH
    angle = jax.random.uniform(key_angle, (FACES, overall_quantity), jnp.float32, -math.pi, math.pi)
    height = jax.random.uniform(key_height, (FACES, overall_quantity), jnp.float32, -1.0, 1.0)
    radial = jnp.sqrt(jnp.maximum(1.0 - height * height, 0.0))
    return jnp.stack([radial * jnp.cos(angle), radial * jnp.sin(angle), height], 0)


def draw_neighbor(key, part):
    key = jax.random.fold_in(key, 11)
    seed_handles = jax.random.split(key, 4)
    overall_quantity = CELL_DEV * N_MESH
    owner = jnp.arange(overall_quantity, dtype=jnp.int32) // CELL_DEV
    face_kind = jax.random.randint(seed_handles[0], (FACES, overall_quantity), 0, 20)
    local_cell = jax.random.randint(seed_handles[1], (FACES, overall_quantity), 0, CELL_DEV)
    source_part = (owner[None, :] + jax.random.randint(seed_handles[2], (FACES, overall_quantity), 1, N_MESH)) % N_MESH
    slot_index = jax.random.randint(seed_handles[3], (FACES, overall_quantity), 0, HALO)
    remote = CELL_DEV + source_part * HALO + slot_index
    boundary = CELL_DEV + N_MESH * HALO
    result = jnp.where(face_kind < 10, local_cell, jnp.where(face_kind < 17, remote, boundary))
    result = result.at[0, 0].set(boundary).at[1, 0].set(0)
    return result.astype(jnp.int32)


def plant(entries, own_key, smallest, high):
    shape = entries.shape
    index_at = [jax.random.randint(jax.random.fold_in(own_key, axis), (), 0, shape[axis]) for axis in range(len(shape))]
    entries = entries.at[tuple(index_at)].set(smallest)
    longest = shape.index(max(shape))
    index_at[longest] = (index_at[longest] + 1) % shape[longest]
    return entries.at[tuple(index_at)].set(high)


def level_of(own_key, extent, shards, least, top_value):
    gain = 1.0
    for axis_at, parts in shards:
        draws = jax.random.uniform(jax.random.fold_in(jax.random.fold_in(own_key, 6), axis_at), (parts,), jnp.float32, least / len(shards), top_value / len(shards))
        gain = gain * jnp.repeat(jnp.exp(draws), extent[axis_at] // parts).reshape((-1,) + (1,) * (len(extent) - 1 - axis_at))
    return gain


def setup_inputs(seed: int = 0) -> dict:
    seeds = jax.random.split(jax.random.key(seed), 8)
    return {
        "dist_old": draw_dist_old(jax.random.fold_in(seeds[7], 71), 0),
        "volume": jnp.clip(jnp.exp(math.log(2.0) - 1.3862944 * jax.random.uniform(seeds[1], (CELLS,), jnp.float32) ** level_of(seeds[1], (CELLS,), ((0, 8),), -0.2, 0.2)), 0.5, 2.0),
        "area": jnp.clip(jnp.exp(math.log(1.5) - 1.60943787 * jax.random.uniform(seeds[2], (FACES, CELLS), jnp.float32) ** level_of(seeds[2], (FACES, CELLS), ((1, 8),), -0.2, 0.2)), 0.3, 1.5),
        "normals": draw_normals(jax.random.fold_in(seeds[7], 71), 0),
        "neighbor": draw_neighbor(jax.random.fold_in(seeds[7], 71), 0),
        "union_rows": plant(jax.random.randint(seeds[5], (N_MESH, UNION), 0, CELL_DEV), jax.random.fold_in(seeds[5], 1), 0, CELL_DEV - 1).astype(jnp.int32),
        "union_index": plant(jax.random.randint(seeds[6], (N_MESH, N_MESH, HALO), 0, UNION), jax.random.fold_in(seeds[6], 1), 0, UNION - 1).astype(jnp.int32),
    }


SPEED_LIMIT = 10.0
TIME_STEP = 0.5
MU_REF = 0.5
VISC_EXPONENT = 0.81
DIFFUSIVITY_RAT = 2.0 / 3.0
INFLOW_SPEED = 5.0


def grid_coords(start, count):
    index = start + jnp.arange(count, dtype=jnp.int32)
    spacing = 2.0 * SPEED_LIMIT / VGRID
    first = index // (VGRID * VGRID)
    second = (index // VGRID) % VGRID
    third = index % VGRID

    def place(level):
        return (level.astype(jnp.float32) + 0.5) * spacing - SPEED_LIMIT

    return place(first), place(second), place(third)


def node_weight():
    spacing = 2.0 * SPEED_LIMIT / VGRID
    return spacing ** 3 / (2.0 * math.pi) ** 1.5


def relative(speeds, center):
    return tuple(speeds[axis_index][None, :] - center[axis_index][:, None] for axis_index in range(3))


def low_sums(dist, speeds, center):
    weighted = dist * node_weight()
    rel_x, rel_y, rel_z = relative(speeds, center)
    return jnp.stack([jnp.sum(weighted, 1), jnp.sum(weighted * rel_x, 1), jnp.sum(weighted * rel_y, 1), jnp.sum(weighted * rel_z, 1)])


def high_sums(dist, speeds, center):
    weighted = dist * node_weight()
    rel_x, rel_y, rel_z = relative(speeds, center)
    energy = weighted * (rel_x * rel_x + rel_y * rel_y + rel_z * rel_z)
    return jnp.stack([jnp.sum(weighted * rel_x * rel_x, 1), jnp.sum(weighted * rel_y * rel_y, 1), jnp.sum(weighted * rel_z * rel_z, 1),
                      jnp.sum(weighted * rel_x * rel_y, 1), jnp.sum(weighted * rel_x * rel_z, 1), jnp.sum(weighted * rel_y * rel_z, 1),
                      jnp.sum(energy * rel_x, 1), jnp.sum(energy * rel_y, 1), jnp.sum(energy * rel_z, 1)])


def finish(local_concentration, center, sums):
    shift = sums[1:4] / local_concentration
    mean_flow_vector = center + shift
    shift_x, shift_y, shift_z = shift[0], shift[1], shift[2]
    s_xx, s_yy, s_zz, s_xy, s_xz, s_yz = sums[4], sums[5], sums[6], sums[7], sums[8], sums[9]
    diagonal_pressure_sum = s_xx + s_yy + s_zz
    offset_norm_power = shift_x * shift_x + shift_y * shift_y + shift_z * shift_z
    thermal_level = (diagonal_pressure_sum - local_concentration * offset_norm_power) / (3.0 * local_concentration)
    proj_x = s_xx * shift_x + s_xy * shift_y + s_xz * shift_z
    proj_y = s_xy * shift_x + s_yy * shift_y + s_yz * shift_z
    proj_z = s_xz * shift_x + s_yz * shift_y + s_zz * shift_z
    heat_x = 0.5 * (sums[10] - 2.0 * proj_x - shift_x * diagonal_pressure_sum + 2.0 * local_concentration * offset_norm_power * shift_x)
    heat_y = 0.5 * (sums[11] - 2.0 * proj_y - shift_y * diagonal_pressure_sum + 2.0 * local_concentration * offset_norm_power * shift_y)
    heat_z = 0.5 * (sums[12] - 2.0 * proj_z - shift_z * diagonal_pressure_sum + 2.0 * local_concentration * offset_norm_power * shift_z)
    return jnp.stack([local_concentration, mean_flow_vector[0], mean_flow_vector[1], mean_flow_vector[2], thermal_level,
                      s_xx - local_concentration * shift_x * shift_x, s_yy - local_concentration * shift_y * shift_y, s_zz - local_concentration * shift_z * shift_z,
                      s_xy - local_concentration * shift_x * shift_y, s_xz - local_concentration * shift_x * shift_z, s_yz - local_concentration * shift_y * shift_z,
                      heat_x, heat_y, heat_z])


def two_section(dist, speeds):
    zero_center = jnp.zeros((3, dist.shape[0]), jnp.float32)
    low = low_sums(dist, speeds, zero_center)
    mean_flow_vector = low[1:4] / low[0]
    high = high_sums(dist, speeds, mean_flow_vector)
    return finish(low[0], mean_flow_vector, jnp.concatenate([low[0:1], jnp.zeros_like(mean_flow_vector), high], 0))


def target(cell_moment_table, speeds):
    local_concentration = cell_moment_table[0]
    thermal_level = cell_moment_table[4]
    rel_x, rel_y, rel_z = relative(speeds, cell_moment_table[1:4])
    peculiar_speed_norm = rel_x * rel_x + rel_y * rel_y + rel_z * rel_z
    thermal_entry_index = thermal_level[:, None]
    equilibrium_distribution = (local_concentration * thermal_level ** -1.5)[:, None] * jnp.exp(-peculiar_speed_norm / (2.0 * thermal_entry_index))
    heat_correction_multiplier = ((1.0 - DIFFUSIVITY_RAT) / (5.0 * local_concentration * thermal_level * thermal_level))[:, None]
    conduction_projection = rel_x * cell_moment_table[11][:, None] + rel_y * cell_moment_table[12][:, None] + rel_z * cell_moment_table[13][:, None]
    return equilibrium_distribution * (1.0 + heat_correction_multiplier * conduction_projection * (peculiar_speed_norm / thermal_entry_index - 5.0))


def collision(cell_moment_table):
    return cell_moment_table[0] * cell_moment_table[4] ** (1.0 - VISC_EXPONENT) / MU_REF


def reference(dist_old, volume, area, normals, neighbor, union_rows, union_index):
    overall_quantity = CELL_DEV * N_MESH
    speeds = grid_coords(0, VGRID ** 3)
    speed_x, speed_y, speed_z = speeds
    owner = jnp.arange(overall_quantity, dtype=jnp.int32) // CELL_DEV
    boundary = CELL_DEV + N_MESH * HALO
    owner_row = jnp.broadcast_to(owner[None, :], neighbor.shape)
    offset = jnp.clip(neighbor - CELL_DEV, 0, N_MESH * HALO - 1)
    source_part = offset // HALO
    slot_index = offset % HALO
    sent_row = union_rows[source_part, union_index[source_part, owner_row, slot_index]]
    global_row = jnp.where(neighbor < CELL_DEV, owner_row * CELL_DEV + jnp.clip(neighbor, 0, CELL_DEV - 1),
                           jnp.where(neighbor < boundary, source_part * CELL_DEV + sent_row, overall_quantity)).astype(jnp.int32)
    freestream = jnp.exp(-((speed_x - INFLOW_SPEED) ** 2 + speed_y ** 2 + speed_z ** 2) / 2.0)

    def moments(dist):
        def one_block(block):
            return two_section(block, speeds)
        result = lax.map(one_block, dist.reshape(N_MESH, CELL_DEV, -1))
        return jnp.moveaxis(result, 0, 1).reshape(14, overall_quantity)

    old_blocks = dist_old.reshape(N_MESH, CELL_DEV, -1)
    vol_blocks = volume.reshape(N_MESH, CELL_DEV)
    area_blocks = jnp.moveaxis(area.reshape(FACES, N_MESH, CELL_DEV), 1, 0)
    normal_blocks = jnp.moveaxis(normals.reshape(3, FACES, N_MESH, CELL_DEV), 2, 0)
    row_blocks = jnp.moveaxis(global_row.reshape(FACES, N_MESH, CELL_DEV), 1, 0)
    current = dist_old
    cell_moment_table = moments(current)
    for sweep_index in range(ITERS):
        extended = jnp.concatenate([current, freestream[None, :]], 0)
        field_blocks = jnp.moveaxis(cell_moment_table.reshape(14, N_MESH, CELL_DEV), 1, 0)

        def relax_block(pieces):
            old_block, field_block, vol_block, area_block, normal_block, row_block = pieces
            rate = collision(field_block)
            stay = vol_block / TIME_STEP
            numer = stay[:, None] * old_block + (vol_block * rate)[:, None] * target(field_block, speeds)
            denom = (stay + vol_block * rate)[:, None]
            for face_index in range(FACES):
                normal_speed = (normal_block[0, face_index][:, None] * speed_x[None, :] + normal_block[1, face_index][:, None] * speed_y[None, :]
                                + normal_block[2, face_index][:, None] * speed_z[None, :])
                beyond = jnp.take(extended, row_block[face_index], axis=0)
                numer = numer + area_block[face_index][:, None] * jnp.maximum(-normal_speed, 0.0) * beyond
                denom = denom + area_block[face_index][:, None] * jnp.maximum(normal_speed, 0.0)
            return numer / denom

        current = lax.map(relax_block, (old_blocks, field_blocks, vol_blocks, area_blocks, normal_blocks, row_blocks)).reshape(overall_quantity, -1)
        cell_moment_table = moments(current)
    return current, cell_moment_table
```

```python
import functools
import math

import jax
import jax.numpy as jnp
from jax import lax
from jax.experimental import pallas as pl
from jax.experimental.pallas import tpu as pltpu
from jax.sharding import PartitionSpec as P

VGRID = 64
SPEED_LIMIT = 10.0
TIME_STEP = 0.5
MU_REF = 0.5
VISC_EXPONENT = 0.81
DIFFUSIVITY_RAT = 2.0 / 3.0
INFLOW_SPEED = 5.0
H = 2.0 * SPEED_LIMIT / VGRID
WEIGHT = H**3 / (2.0 * math.pi) ** 1.5

CELL = 32
FACES = 4
LANES = 128
CHUNK = 2048
VEL = 8192
NB = 32
NC = 64
NVEL = 32
PAY = CHUNK + 2 * LANES
VMEM_LIMIT = 48 * 1024 * 1024

R_AREA, R_NORM, R_VOL, R_NEIGH, R_UOWN, R_UPEER, R_PAR = 0, 4, 16, 17, 21, 22, 24


def place(level):
    return (level.astype(jnp.float32) + 0.5) * H - SPEED_LIMIT


def lane_iota(shape):
    return lax.broadcasted_iota(jnp.int32, shape, 1)


def row_iota(shape):
    return lax.broadcasted_iota(jnp.int32, shape, 0)


def rows_sum(x):
    return jnp.sum(x, axis=0, keepdims=True)


def first_kernel(sc, d_ref, par_ref, *outs):
    y = sc[0]
    vel = sc[2]
    par = pltpu.roll(par_ref[...], y * CELL, 1)
    lane = lane_iota((8, LANES))
    par_y = (lane // NC).astype(jnp.float32) * H
    vz = place(lane % NC)
    base_y = par_y + (0.5 * H - SPEED_LIMIT)
    vx = [place(jnp.full((8, LANES), 2 * vel + a, jnp.int32)) for a in range(2)]
    tiles = []
    for group in range(4):
        rows = slice(8 * group, 8 * group + 8)
        a0 = [None, None]
        a1 = None
        for a in range(2):
            for t in range(32):
                x = d_ref[rows, pl.ds((a * 32 + t) * LANES, LANES)]
                a0[a] = x if t == 0 else a0[a] + x
                if t:
                    a1 = x * float(t) if a1 is None else a1 + x * float(t)
        both = a0[0] + a0[1]
        rho = jnp.sum(both, axis=1, keepdims=True)
        inv = 1.0 / jnp.maximum(rho, 1e-30)

        def mean(total):
            value = jnp.sum(total, axis=1, keepdims=True) * inv
            return jnp.clip(value, -SPEED_LIMIT, SPEED_LIMIT)

        cen_x = mean(a0[0] * vx[0] + a0[1] * vx[1])
        cen_y = mean(a1 * (2.0 * H) + both * base_y)
        cen_z = mean(both * vz)
        cz = vz - cen_z
        cz2 = cz * cz
        start_y = base_y - cen_y
        sums = [None] * 13

        def add(index, value):
            sums[index] = value if sums[index] is None else sums[index] + value

        for a in range(2):
            p = [None] * 4
            for t in range(32):
                x = d_ref[rows, pl.ds((a * 32 + t) * LANES, LANES)]
                cy = start_y + 2.0 * H * t
                for power in range(4):
                    p[power] = x if t == 0 else p[power] + x
                    x = x * cy
            cx = vx[a] - cen_x
            cx2 = cx * cx
            xz0 = (cx2 + cz2) * p[0] + p[2]
            add(0, p[0])
            add(1, cx * p[0])
            add(2, p[1])
            add(3, cz * p[0])
            add(4, cx2 * p[0])
            add(5, p[2])
            add(6, cz2 * p[0])
            add(7, cx * p[1])
            add(8, cx * cz * p[0])
            add(9, cz * p[1])
            add(10, cx * xz0)
            add(11, (cx2 + cz2) * p[1] + p[3])
            add(12, cz * xz0)
        cols = [jnp.sum(s, axis=1, keepdims=True) * WEIGHT for s in sums]
        cols += [cen_x, cen_y, cen_z]
        tile = jnp.zeros((8, LANES), jnp.float32)
        for q, col in enumerate(cols):
            tile = jnp.where(lane == q, col, tile)
        tiles.append(tile)
    square = jnp.concatenate(tiles + [jnp.zeros((LANES - CELL, LANES), jnp.float32)], 0)
    part = pltpu.roll(square.T[0:16], y * CELL, 1)
    for k, out in enumerate(outs):
        chunk = pl.multiple_of((y ^ k) * CHUNK, LANES)
        out[:, 0:CHUNK] = d_ref[:, pl.ds(chunk, CHUNK)]
        out[0:R_PAR, CHUNK : CHUNK + LANES] = par
        out[R_PAR:CELL, CHUNK : CHUNK + LANES] = jnp.zeros((CELL - R_PAR, LANES), jnp.float32)
        out[0:16, CHUNK + LANES : PAY] = part
        out[16:CELL, CHUNK + LANES : PAY] = jnp.zeros((CELL - 16, LANES), jnp.float32)


def face_tables(par, vz):
    scaled = []
    for j in range(FACES):
        area = par[R_AREA + j : R_AREA + j + 1]
        n = [par[R_NORM + 4 * d + j : R_NORM + 4 * d + j + 1] * area for d in range(3)]
        scaled.append(n)
    return scaled


def prepare_kernel(sc, p0, p1, p2, p3, ui_ref, dt_ref, base_ref, out_ref, hot_ref, par_ref, stack, ztab, ftab):
    y, core, plane, first_b = sc[0], sc[1], sc[3], sc[4]
    pays = (p0, p1, p2, p3)
    par = functools.reduce(jnp.add, [p[0:R_PAR, CHUNK : CHUNK + LANES] for p in pays])
    par_ref[...] = par
    for k, p in enumerate(pays):
        row = pl.multiple_of((y ^ k) * CELL, 8)
        stack[pl.ds(row, CELL), :] = p[:, 0:CHUNK]
    for blk in range(CHUNK // LANES):
        cols = slice(blk * LANES, (blk + 1) * LANES)
        dt_ref[cols, :] = stack[:, cols].T

    lane = lane_iota((1, LANES))
    own_rows = jnp.broadcast_to(par[R_UOWN : R_UOWN + 1], (LANES, LANES)).T
    peer_rows = jnp.broadcast_to(par[R_UPEER : R_UPEER + 1], (LANES, LANES)).T
    slots = row_iota((64, LANES))
    entries = row_iota((LANES, LANES))
    masks = []
    for j in range(FACES):
        e = par[R_NEIGH + j : R_NEIGH + j + 1].astype(jnp.int32)
        off = jnp.clip(e - CELL, 0, 63)
        source = off // 8
        position = rows_sum(jnp.where(slots == off, ui_ref[...], 0))
        entry = (source // 2) * CELL + position
        mine = (source % 2) == core
        found = jnp.where(entries == entry, jnp.where(mine, own_rows, peer_rows), 0.0)
        remote = rows_sum(found).astype(jnp.int32) + (source // 2) * CELL + jnp.where(mine, 0, LANES)
        local_row = (lane // CELL) * CELL + e
        target = jnp.where(e < CELL, local_row, jnp.where(e < CELL + 64, remote, -1))
        hot = (row_iota((2 * LANES, LANES)) == target).astype(jnp.float32)
        hot_ref[:, j * LANES : (j + 1) * LANES] = hot.astype(jnp.bfloat16)
        masks.append((e >= CELL + 64).astype(jnp.float32))

    vz = place(row_iota((NC, LANES)))
    scaled = face_tables(par, vz)
    for j in range(FACES):
        ztab[j] = scaled[j][2] * vz
    ftab[...] = jnp.exp(-0.5 * vz * vz)
    vx = place(jnp.full((1, LANES), plane, jnp.int32))
    stay = par[R_VOL : R_VOL + 1] / TIME_STEP

    def body(b, _):
        vy = place(jnp.full((1, LANES), first_b + b, jnp.int32))
        free = jnp.exp(-0.5 * ((vx - INFLOW_SPEED) ** 2 + vy * vy))
        xy = [scaled[j][0] * vx + scaled[j][1] * vy for j in range(FACES)]
        for ct in range(NC // 8):
            rows = pl.ds(pl.multiple_of(b * NC + ct * 8, 8), 8)
            outflow = jnp.zeros((8, LANES), jnp.float32)
            inflow = jnp.zeros((8, LANES), jnp.float32)
            for j in range(FACES):
                s = xy[j] + ztab[j, ct * 8 : ct * 8 + 8]
                outflow = outflow + jnp.maximum(s, 0.0)
                inflow = inflow + jnp.maximum(-s, 0.0) * masks[j]
            out_ref[rows, :] = outflow
            base_ref[rows, :] = stay * dt_ref[rows, :] + (free * ftab[ct * 8 : ct * 8 + 8]) * inflow
        return 0

    lax.fori_loop(0, NB, body, 0)


def faces_kernel(sc, f_ref, g_ref, base_ref, hot_ref, par_ref, num_ref, ztab):
    plane, first_b = sc[3], sc[4]
    par = par_ref[...]
    vz = place(row_iota((NC, LANES)))
    scaled = face_tables(par, vz)
    for j in range(FACES):
        ztab[j] = scaled[j][2] * vz
    vx = place(jnp.full((1, LANES), plane, jnp.int32))
    step_b = 4
    size = step_b * NC

    def body(it, _):
        rows = pl.ds(pl.multiple_of(it * size, size), size)
        x = jnp.concatenate([f_ref[rows, :], g_ref[rows, :]], 1)
        high = x.astype(jnp.bfloat16)
        low = (x - high.astype(jnp.float32)).astype(jnp.bfloat16)
        hot = hot_ref[...]
        got = jnp.dot(high, hot, preferred_element_type=jnp.float32)
        got = got + jnp.dot(low, hot, preferred_element_type=jnp.float32)
        for bb in range(step_b):
            vy = place(jnp.full((1, LANES), first_b + it * step_b + bb, jnp.int32))
            total = base_ref[pl.ds(pl.multiple_of(it * size + bb * NC, NC), NC), :]
            for j in range(FACES):
                xy = scaled[j][0] * vx + scaled[j][1] * vy
                s = xy + ztab[j]
                total = total - jnp.minimum(s, 0.0) * got[bb * NC : (bb + 1) * NC, j * LANES : (j + 1) * LANES]
            num_ref[pl.ds(pl.multiple_of(it * size + bb * NC, NC), NC), :] = total
        return 0

    lax.fori_loop(0, NB // step_b, body, 0)


def finish_rows(rho, center, s):
    sh = [s[i] / rho for i in (1, 2, 3)]
    mean = [center[i] + sh[i] for i in range(3)]
    xx, yy, zz, xy, xz, yz = s[4:10]
    trace = xx + yy + zz
    norm = sh[0] * sh[0] + sh[1] * sh[1] + sh[2] * sh[2]
    temp = (trace - rho * norm) / (3.0 * rho)
    proj = [
        xx * sh[0] + xy * sh[1] + xz * sh[2],
        xy * sh[0] + yy * sh[1] + yz * sh[2],
        xz * sh[0] + yz * sh[1] + zz * sh[2],
    ]
    heat = [0.5 * (s[10 + i] - 2.0 * proj[i] - sh[i] * trace + 2.0 * rho * norm * sh[i]) for i in range(3)]
    stress = [
        xx - rho * sh[0] * sh[0],
        yy - rho * sh[1] * sh[1],
        zz - rho * sh[2] * sh[2],
        xy - rho * sh[0] * sh[1],
        xz - rho * sh[0] * sh[2],
        yz - rho * sh[1] * sh[2],
    ]
    return [rho] + mean + [temp] + stress + heat


def moments_first(part_ref):
    q = [part_ref[:, i, :] for i in range(16)]
    rho_d, m, s, heat, cen = q[0], q[1:4], q[4:10], q[10:13], q[13:16]
    rho = rows_sum(rho_d)
    u = [rows_sum(m[i] + rho_d * cen[i]) / rho for i in range(3)]
    d = [cen[i] - u[i] for i in range(3)]
    tensor = ((0, 3, 4), (3, 1, 5), (4, 5, 2))
    pairs = ((0, 0), (1, 1), (2, 2), (0, 1), (0, 2), (1, 2))
    d2 = d[0] * d[0] + d[1] * d[1] + d[2] * d[2]
    m_d = m[0] * d[0] + m[1] * d[1] + m[2] * d[2]
    total = s[0] + s[1] + s[2] + 2.0 * m_d + rho_d * d2
    sums = [rho] + [rows_sum(m[i] + rho_d * d[i]) for i in range(3)]
    for n, (i, j) in enumerate(pairs):
        sums.append(rows_sum(s[n] + m[i] * d[j] + d[i] * m[j] + rho_d * d[i] * d[j]))
    for i in range(3):
        along = s[tensor[i][0]] * d[0] + s[tensor[i][1]] * d[1] + s[tensor[i][2]] * d[2]
        sums.append(rows_sum(heat[i] + 2.0 * along + m[i] * d2 + d[i] * total))
    return finish_rows(rho, u, sums)


def moments_next(part_ref, cen_ref):
    total = part_ref[0]
    for n in range(1, NVEL):
        total = total + part_ref[n]
    s = [total[i : i + 1] for i in range(13)]
    return finish_rows(s[0], [cen_ref[i : i + 1] for i in range(3)], s)


def relax(sc, moments, num_ref, out_ref, par_ref, store, part_ref, cen_ref, tabs):
    zt_ref, zq_ref, zg_ref, cz_ref = tabs
    plane, first_b = sc[3], sc[4]
    rho, ux, uy, uz, temp = moments[0:5]
    heat = moments[11:14]
    vol = par_ref[R_VOL : R_VOL + 1]
    log_t = jnp.log(temp)
    rate = rho * jnp.exp((1.0 - VISC_EXPONENT) * log_t) * (1.0 / MU_REF)
    volrate = vol * rate
    fixed = vol / TIME_STEP + volrate
    scale = volrate * rho * jnp.exp(-1.5 * log_t)
    inv_t = 1.0 / temp
    mult = (1.0 - DIFFUSIVITY_RAT) / (5.0 * rho * temp * temp)
    heat = [mult * h for h in heat]
    cx = place(jnp.full((1, LANES), plane, jnp.int32)) - ux
    cx2 = cx * cx
    cz = place(row_iota((NC, LANES))) - uz
    cz_ref[...] = cz
    zt = cz * cz * inv_t
    zt_ref[...] = zt
    zg_ref[...] = jnp.exp(-0.5 * zt)
    zq_ref[...] = cz * heat[2]
    x_t = cx2 * inv_t
    x_q = cx * heat[0]
    zero = jnp.zeros((8, LANES), jnp.float32)

    def body(b, acc):
        cy = place(jnp.full((1, LANES), first_b + b, jnp.int32)) - uy
        cy2 = cy * cy
        xy_t = x_t + cy2 * inv_t
        xy_g = scale * jnp.exp(-0.5 * xy_t)
        xy_t = xy_t - 5.0
        xy_q = x_q + cy * heat[1]
        p = [None] * 4
        for ct in range(NC // 8):
            loc = slice(ct * 8, ct * 8 + 8)
            rows = pl.ds(pl.multiple_of(b * NC + ct * 8, 8), 8)
            poly = 1.0 + (xy_q + zq_ref[loc]) * (xy_t + zt_ref[loc])
            num = num_ref[rows, :] + (xy_g * zg_ref[loc]) * poly
            f = num / (fixed + out_ref[rows, :])
            store(rows, f)
            c = cz_ref[loc]
            for power in range(4):
                p[power] = f if p[power] is None else p[power] + f
                if power < 3:
                    f = f * c
        new = [
            p[0], cy * p[0], cy2 * p[0], cy2 * cy * p[0],
            p[1], cy * p[1], cy2 * p[1],
            p[2], cy * p[2],
            p[3],
        ]
        return tuple(o + n for o, n in zip(acc, new))

    acc = lax.fori_loop(0, NB, body, (zero,) * 10)
    t0, t0y, t0yy, t0yyy, t1, t1y, t1yy, t2, t2y, t3 = [rows_sum(a) * WEIGHT for a in acc]
    rows = [
        t0, cx * t0, t0y, t1,
        cx2 * t0, t0yy, t2, cx * t0y, cx * t1, t1y,
        cx * (cx2 * t0 + t0yy + t2),
        cx2 * t0y + t0yyy + t2y,
        cx2 * t1 + t1yy + t3,
    ]
    for i, row in enumerate(rows):
        part_ref[i : i + 1] = row
    part_ref[13:16] = jnp.zeros((3, LANES), jnp.float32)
    for i, row in enumerate((ux, uy, uz)):
        cen_ref[i : i + 1] = row
    cen_ref[3:8] = jnp.zeros((5, LANES), jnp.float32)


def relax_first_kernel(sc, parts, num_ref, out_ref, par_ref, f_ref, part_ref, cen_ref, *tabs):
    def store(rows, f):
        f_ref[rows, :] = f

    relax(sc, moments_first(parts), num_ref, out_ref, par_ref, store, part_ref, cen_ref, tabs)


def relax_next_kernel(sc, parts, num_ref, out_ref, par_ref, old_ref, f_ref, part_ref, cen_ref, *tabs):
    def store(rows, f):
        f_ref[rows, :] = f

    relax(sc, moments_next(parts, old_ref), num_ref, out_ref, par_ref, store, part_ref, cen_ref, tabs)


def relax_last_kernel(sc, parts, num_ref, out_ref, par_ref, old_ref, o0, o1, o2, o3, part_ref, cen_ref, *scratch):
    tabs, f_ref, stack = scratch[0:4], scratch[4], scratch[5]
    y = sc[0]

    def store(rows, f):
        f_ref[rows, :] = f

    relax(sc, moments_next(parts, old_ref), num_ref, out_ref, par_ref, store, part_ref, cen_ref, tabs)
    for blk in range(CHUNK // LANES):
        cols = slice(blk * LANES, (blk + 1) * LANES)
        stack[:, cols] = f_ref[cols, :].T
    for k, o in enumerate((o0, o1, o2, o3)):
        row = pl.multiple_of((y ^ k) * CELL, 8)
        o[...] = stack[pl.ds(row, CELL), :]


def table_kernel(sc, parts, cen_ref, table_ref):
    y = sc[0]
    rows = moments_next(parts, cen_ref)
    full = jnp.concatenate(rows + [jnp.zeros((2, LANES), jnp.float32)], 0)
    full = pltpu.roll(full, (LANES - y * CELL) % LANES, 1)
    table_ref[...] = full[0:14, 0:CELL]


def assemble_kernel(sc, r0, r1, r2, r3, out):
    y = sc[0]
    for k, r in enumerate((r0, r1, r2, r3)):
        out[:, pl.ds(pl.multiple_of((y ^ k) * CHUNK, LANES), CHUNK)] = r[...]


def call(kernel, name, n_in, out_shapes, scratch=(), flops=10_000_000):
    vmem = pl.BlockSpec(memory_space=pltpu.VMEM)
    return pl.pallas_call(
        kernel,
        name=name,
        out_shape=out_shapes,
        in_specs=[pl.BlockSpec(memory_space=pltpu.SMEM)] + [vmem] * n_in,
        out_specs=jax.tree.map(lambda _: vmem, out_shapes),
        scratch_shapes=list(scratch),
        compiler_params=pltpu.CompilerParams(vmem_limit_bytes=VMEM_LIMIT),
        cost_estimate=pl.CostEstimate(flops=flops, bytes_accessed=4_000_000, transcendentals=100_000),
    )


def f32(*shape):
    return jax.ShapeDtypeStruct(shape, jnp.float32)


def toward_y(values):
    out = [values[0]]
    for k in (1, 3, 2):
        out.append(lax.ppermute(values[k], "mesh", [(m, m ^ (2 * k)) for m in range(8)]))
    return [out[0], out[1], out[3], out[2]]


def other_core(value):
    return lax.ppermute(value, "mesh", [(m, m ^ 1) for m in range(8)])


def spread(part):
    return lax.all_to_all(jnp.broadcast_to(part[None], (NVEL, 16, LANES)), "vel", 0, 0)


def local(dist_old, volume, area, normals, neighbor, union_rows, union_index):
    vel = lax.axis_index("vel")
    m = lax.axis_index("mesh")
    y, core = m // 2, m % 2
    sc = jnp.stack([y, core, vel, 2 * vel + y // 2, NB * (y % 2)]).astype(jnp.int32)
    union_f = union_rows.astype(jnp.float32)
    union_peer = other_core(union_f)
    par = jnp.concatenate(
        [
            area,
            normals.reshape(3 * FACES, CELL),
            volume[None],
            neighbor.astype(jnp.float32),
            jnp.pad(union_f, ((0, 0), (0, CELL - 16))),
            jnp.pad(union_peer, ((0, 0), (0, CELL - 16))),
            jnp.zeros((1, CELL), jnp.float32),
        ],
        0,
    )
    par = jnp.pad(par, ((0, 0), (0, LANES - CELL)))
    mine = lax.dynamic_index_in_dim(union_index.reshape(8, 4, 2, 8), core, 2, keepdims=False)
    slots = jnp.repeat(jnp.transpose(mine, (0, 2, 1)).reshape(64, 4), CELL, axis=1)

    pays = call(first_kernel, "first", 2, (f32(CELL, PAY),) * 4)(sc, dist_old, par)
    got = toward_y(pays)
    part = functools.reduce(jnp.add, [g[0:16, CHUNK + LANES :] for g in got])
    parts = spread(part)
    state = f32(CHUNK, LANES)
    d_t, base, outflow, hot, par = call(
        prepare_kernel,
        "prepare",
        5,
        (state, state, state, jax.ShapeDtypeStruct((2 * LANES, FACES * LANES), jnp.bfloat16), f32(R_PAR, LANES)),
        (
            pltpu.VMEM((LANES, CHUNK), jnp.float32),
            pltpu.VMEM((FACES, NC, LANES), jnp.float32),
            pltpu.VMEM((NC, LANES), jnp.float32),
        ),
    )(sc, *got, slots)
    tabs = (pltpu.VMEM((NC, LANES), jnp.float32),) * 4
    faces = call(
        faces_kernel, "faces", 5, state, (pltpu.VMEM((FACES, NC, LANES), jnp.float32),), flops=100_000_000
    )
    small = (f32(16, LANES), f32(8, LANES))

    num = faces(sc, d_t, other_core(d_t), base, hot, par)
    f, part, cen = call(relax_first_kernel, "relax_first", 4, (state,) + small, tabs)(
        sc, parts, num, outflow, par
    )
    part = functools.reduce(jnp.add, toward_y([part] * 4))
    parts = spread(part)
    num = faces(sc, f, other_core(f), base, hot, par)
    f, part, cen = call(relax_next_kernel, "relax_next", 5, (state,) + small, tabs)(
        sc, parts, num, outflow, par, cen
    )
    part = functools.reduce(jnp.add, toward_y([part] * 4))
    parts = spread(part)
    num = faces(sc, f, other_core(f), base, hot, par)
    *chunks, part, cen = call(
        relax_last_kernel,
        "relax_last",
        5,
        (f32(CELL, CHUNK),) * 4 + small,
        tabs + (pltpu.VMEM((CHUNK, LANES), jnp.float32), pltpu.VMEM((LANES, CHUNK), jnp.float32)),
    )(sc, parts, num, outflow, par, cen)
    part = functools.reduce(jnp.add, toward_y([part] * 4))
    part, chunks = lax.optimization_barrier((part, chunks))
    blocks = toward_y(chunks)
    parts = spread(part)
    dist_new = call(assemble_kernel, "assemble", 4, f32(CELL, VEL))(sc, *blocks)
    table = call(table_kernel, "table", 2, f32(14, CELL))(sc, parts, cen)
    return dist_new, table


def solution(mesh):
    placed = (
        P("mesh", "vel"),
        P("mesh"),
        P(None, "mesh"),
        P(None, None, "mesh"),
        P(None, "mesh"),
        P("mesh", None),
        P(),
    )
    return jax.shard_map(
        local,
        mesh=mesh,
        in_specs=placed,
        out_specs=(P("mesh", "vel"), P(None, "mesh")),
        check_vma=False,
    )
```

```python
import functools
import math

import jax
import jax.numpy as jnp
from jax import lax
from jax.experimental import pallas as pl
from jax.experimental.pallas import tpu as pltpu
from jax.sharding import PartitionSpec as P

VGRID = 64
SPEED_LIMIT = 10.0
TIME_STEP = 0.5
MU_REF = 0.5
VISC_EXPONENT = 0.81
DIFFUSIVITY_RAT = 2.0 / 3.0
INFLOW_SPEED = 5.0
H = 2.0 * SPEED_LIMIT / VGRID
WEIGHT = H**3 / (2.0 * math.pi) ** 1.5

CELL = 32
FACES = 4
LANES = 128
CHUNK = 2048
VEL = 8192
NB = 32
NC = 64
NVEL = 32
PIECES = 4
PAY = CHUNK + LANES
NSRC = 4 * NVEL
VMEM_LIMIT = 12 * 1024 * 1024
SMALL_LIMIT = 4 * 1024 * 1024

R_AREA, R_NORM, R_VOL, R_NEIGH, R_UNION, R_PAR = 0, 4, 16, 17, 21, 24


def place(level):
    return (level.astype(jnp.float32) + 0.5) * H - SPEED_LIMIT


def lane_iota(shape):
    return lax.broadcasted_iota(jnp.int32, shape, 1)


def row_iota(shape):
    return lax.broadcasted_iota(jnp.int32, shape, 0)


def rows_sum(x):
    return jnp.sum(x, axis=0, keepdims=True)


def pack(part, block):
    lane = lane_iota((4, LANES)) // CELL
    out = jnp.zeros((4, LANES), jnp.float32)
    for g in range(4):
        shift = CELL * ((g - block) % 4)
        rows = part[4 * g : 4 * g + 4]
        out = jnp.where(lane == g, pltpu.roll(rows, shift, 1) if shift else rows, out)
    return out


def first_kernel(sc, dist, area, normals, volume, neighbor, union, *refs):
    outs, packed, (d_ref, par_ref, sems), small = refs[0:4], refs[4], refs[5:8], refs[8:13]
    pairs = list(zip((area, normals, volume, neighbor, union), small))
    params = [pltpu.make_async_copy(a, b, sems.at[4 + i]) for i, (a, b) in enumerate(pairs)]
    for copy in params:
        copy.start()
    copies = []
    for group in range(4):
        rows = pl.ds(8 * group, 8)
        copies.append(pltpu.make_async_copy(dist.at[rows], d_ref.at[rows], sems.at[group]))
        copies[-1].start()
    y = sc[0]
    vel = sc[2]
    par_ref[...] = jnp.zeros((R_PAR, LANES), jnp.float32)
    for copy in params:
        copy.wait()
    area, normals, volume, neighbor, union = small
    par_ref[R_AREA : R_AREA + FACES, 0:CELL] = area[...]
    for d in range(3):
        par_ref[R_NORM + FACES * d : R_NORM + FACES * (d + 1), 0:CELL] = normals[d]
    par_ref[R_VOL : R_VOL + 1, 0:CELL] = volume[...]
    par_ref[R_NEIGH : R_NEIGH + FACES, 0:CELL] = neighbor[...].astype(jnp.float32)
    par_ref[R_UNION : R_UNION + 1, 0:16] = union[...].astype(jnp.float32)
    par = pltpu.roll(par_ref[...], y * CELL, 1)
    for out in outs:
        out[0:R_PAR, CHUNK:PAY] = par
        out[R_PAR:CELL, CHUNK:PAY] = jnp.zeros((CELL - R_PAR, LANES), jnp.float32)
    lane = lane_iota((8, LANES))
    par_y = (lane // NC).astype(jnp.float32) * H
    vz = place(lane % NC)
    base_y = par_y + (0.5 * H - SPEED_LIMIT)
    vx = [place(jnp.full((8, LANES), 2 * vel + a, jnp.int32)) for a in range(2)]
    wait_all(copies)
    centers = []
    for group in range(4):
        rows = slice(8 * group, 8 * group + 8)
        a0 = [None, None]
        a1 = None
        for a in range(2):
            for t in range(32):
                x = d_ref[rows, pl.ds((a * 32 + t) * LANES, LANES)]
                a0[a] = x if t == 0 else a0[a] + x
                if t:
                    a1 = x * float(t) if a1 is None else a1 + x * float(t)
        both = a0[0] + a0[1]
        totals = [both, a0[0] * vx[0] + a0[1] * vx[1], a1 * (2.0 * H) + both * base_y, both * vz]
        rho, *first = [jnp.sum(total, axis=1, keepdims=True) for total in totals]
        inv = 1.0 / jnp.maximum(rho, 1e-30)
        centers.append([jnp.clip(total * inv, -SPEED_LIMIT, SPEED_LIMIT) for total in first])
    tiles = []
    for group in range(4):
        rows = slice(8 * group, 8 * group + 8)
        cen_x, cen_y, cen_z = centers[group]
        cz = vz - cen_z
        cz2 = cz * cz
        start_y = base_y - cen_y
        sums = [None] * 13

        def add(index, value):
            sums[index] = value if sums[index] is None else sums[index] + value

        for a in range(2):
            p = [None] * 4
            for t in range(32):
                x = d_ref[rows, pl.ds((a * 32 + t) * LANES, LANES)]
                cy = start_y + 2.0 * H * t
                for power in range(4):
                    p[power] = x if t == 0 else p[power] + x
                    if power < 3:
                        x = x * cy
            cx = vx[a] - cen_x
            cx2 = cx * cx
            xz0 = (cx2 + cz2) * p[0] + p[2]
            add(0, p[0])
            add(1, cx * p[0])
            add(2, p[1])
            add(3, cz * p[0])
            add(4, cx2 * p[0])
            add(5, p[2])
            add(6, cz2 * p[0])
            add(7, cx * p[1])
            add(8, cx * cz * p[0])
            add(9, cz * p[1])
            add(10, cx * xz0)
            add(11, (cx2 + cz2) * p[1] + p[3])
            add(12, cz * xz0)
        cols = [jnp.sum(s, axis=1, keepdims=True) * WEIGHT for s in sums]
        cols += [cen_x, cen_y, cen_z]
        tile = jnp.zeros((8, LANES), jnp.float32)
        for q, col in enumerate(cols):
            tile = jnp.where(lane == q, col, tile)
        tiles.append(tile)
    for k, out in enumerate(outs):
        chunk = pl.multiple_of((y ^ k) * CHUNK, LANES)
        out[:, 0:CHUNK] = d_ref[:, pl.ds(chunk, CHUNK)]
    square = jnp.concatenate(tiles + [jnp.zeros((LANES - CELL, LANES), jnp.float32)], 0)
    block = pack(square.T[0:16], 0)
    for n in range(NSRC):
        packed[n] = block


def face_tables(par, vz):
    scaled = []
    for j in range(FACES):
        area = par[R_AREA + j : R_AREA + j + 1]
        n = [par[R_NORM + 4 * d + j : R_NORM + 4 * d + j + 1] * area for d in range(3)]
        scaled.append(n)
    return scaled


def start_all(pairs, sems):
    copies = [pltpu.make_async_copy(a, b, sems.at[i]) for i, (a, b) in enumerate(pairs)]
    for copy in copies:
        copy.start()
    return copies


def wait_all(copies):
    for copy in copies:
        copy.wait()


def to_lanes(stack, out):
    for blk in range(CHUNK // LANES):
        cols = slice(blk * LANES, (blk + 1) * LANES)
        out[cols, :] = stack[:, cols].T


def params_of(blocks):
    return functools.reduce(jnp.add, [blocks[n * CELL : n * CELL + R_PAR, CHUNK : CHUNK + LANES] for n in range(4)])


def prepare_kernel(sc, p0, p1, p2, p3, q0, q1, q2, q3, ui_ref, base, out_ref, num_ref, hot, par_ref, *scratch):
    pays, peers, dt_ref, gt_ref, ztab, ftab, sems, base_ref, hot_ref = scratch
    y, plane, first_b = sc[0], sc[3], sc[4]
    pairs = []
    for stack, blocks in ((pays, (p0, p1, p2, p3)), (peers, (q0, q1, q2, q3))):
        for k, block in enumerate(blocks):
            row = pl.multiple_of((y ^ k) * CELL, 8)
            pairs.append((block, stack.at[pl.ds(row, CELL)]))
    wait_all(start_all(pairs, sems))
    par = params_of(pays)
    par_ref[...] = par
    to_lanes(pays, dt_ref)
    to_lanes(peers, gt_ref)
    gather_table(sc, par, params_of(peers)[R_UNION : R_UNION + 1], ui_ref, hot_ref)
    masks = [(par[R_NEIGH + j : R_NEIGH + j + 1] >= CELL + 64 - 0.5).astype(jnp.float32) for j in range(FACES)]
    vz = place(row_iota((NC, LANES)))
    scaled = face_tables(par, vz)
    for j in range(FACES):
        ztab[j] = scaled[j][2] * vz
    ftab[...] = jnp.exp(-0.5 * vz * vz)
    vx = place(jnp.full((1, LANES), plane, jnp.int32))
    stay = par[R_VOL : R_VOL + 1] / TIME_STEP

    def body(b, _):
        vy = place(jnp.full((1, LANES), first_b + b, jnp.int32))
        free = jnp.exp(-0.5 * ((vx - INFLOW_SPEED) ** 2 + vy * vy))
        xy = [scaled[j][0] * vx + scaled[j][1] * vy for j in range(FACES)]
        for ct in range(NC // 8):
            rows = pl.ds(pl.multiple_of(b * NC + ct * 8, 8), 8)
            outflow = jnp.zeros((8, LANES), jnp.float32)
            inflow = jnp.zeros((8, LANES), jnp.float32)
            for j in range(FACES):
                s = xy[j] + ztab[j, ct * 8 : ct * 8 + 8]
                outflow = outflow + jnp.maximum(s, 0.0)
                inflow = inflow + jnp.maximum(-s, 0.0) * masks[j]
            out_ref[rows, :] = outflow
            base_ref[rows, :] = stay * dt_ref[rows, :] + (free * ftab[ct * 8 : ct * 8 + 8]) * inflow
        return 0

    lax.fori_loop(0, NB, body, 0)
    sends = start_all(((base_ref, base), (hot_ref, hot)), sems)
    faces(sc, dt_ref, gt_ref, base_ref, hot_ref, par_ref, num_ref, ztab)
    wait_all(sends)


def gather_table(sc, par, peer, ui_ref, hot_ref):
    core = sc[1]
    lane = lane_iota((1, LANES))
    own_rows = jnp.broadcast_to(par[R_UNION : R_UNION + 1], (LANES, LANES)).T
    peer_rows = jnp.broadcast_to(peer, (LANES, LANES)).T
    slots = row_iota((64, LANES))
    entries = row_iota((LANES, LANES))
    for j in range(FACES):
        e = par[R_NEIGH + j : R_NEIGH + j + 1].astype(jnp.int32)
        off = jnp.clip(e - CELL, 0, 63)
        source = off // 8
        position = rows_sum(jnp.where(slots == off, ui_ref[...], 0))
        entry = (source // 2) * CELL + position
        mine = (source % 2) == core
        found = jnp.where(entries == entry, jnp.where(mine, own_rows, peer_rows), 0.0)
        remote = rows_sum(found).astype(jnp.int32) + (source // 2) * CELL + jnp.where(mine, 0, LANES)
        local_row = (lane // CELL) * CELL + e
        target = jnp.where(e < CELL, local_row, jnp.where(e < CELL + 64, remote, -1))
        hot = (row_iota((2 * LANES, LANES)) == target).astype(jnp.float32)
        hot_ref[:, j * LANES : (j + 1) * LANES] = hot.astype(jnp.bfloat16)


def faces_kernel(sc, f, g, base, hot, par_ref, num_ref, ztab, f_ref, g_ref, base_ref, hot_ref, sems):
    wait_all(start_all(((f, f_ref), (g, g_ref), (base, base_ref), (hot, hot_ref)), sems))
    faces(sc, f_ref, g_ref, base_ref, hot_ref, par_ref, num_ref, ztab)


def faces(sc, f_ref, g_ref, base_ref, hot_ref, par_ref, num_ref, ztab):
    plane, first_b = sc[3], sc[4]
    par = par_ref[...]
    vz = place(row_iota((NC, LANES)))
    scaled = face_tables(par, vz)
    for j in range(FACES):
        ztab[j] = scaled[j][2] * vz
    vx = place(jnp.full((1, LANES), plane, jnp.int32))
    step_b = 4
    size = step_b * NC

    def body(it, _):
        rows = pl.ds(pl.multiple_of(it * size, size), size)
        x = jnp.concatenate([f_ref[rows, :], g_ref[rows, :]], 1)
        high = x.astype(jnp.bfloat16)
        low = (x - high.astype(jnp.float32)).astype(jnp.bfloat16)
        hot = hot_ref[...]
        got = jnp.dot(high, hot, preferred_element_type=jnp.float32)
        got = got + jnp.dot(low, hot, preferred_element_type=jnp.float32)
        for bb in range(step_b):
            vy = place(jnp.full((1, LANES), first_b + it * step_b + bb, jnp.int32))
            total = base_ref[pl.ds(pl.multiple_of(it * size + bb * NC, NC), NC), :]
            for j in range(FACES):
                xy = scaled[j][0] * vx + scaled[j][1] * vy
                s = xy + ztab[j]
                total = total - jnp.minimum(s, 0.0) * got[bb * NC : (bb + 1) * NC, j * LANES : (j + 1) * LANES]
            num_ref[pl.ds(pl.multiple_of(it * size + bb * NC, NC), NC), :] = total
        return 0

    lax.fori_loop(0, NB // step_b, body, 0)


def finish_rows(rho, center, s):
    sh = [s[i] / rho for i in (1, 2, 3)]
    mean = [center[i] + sh[i] for i in range(3)]
    xx, yy, zz, xy, xz, yz = s[4:10]
    trace = xx + yy + zz
    norm = sh[0] * sh[0] + sh[1] * sh[1] + sh[2] * sh[2]
    temp = (trace - rho * norm) / (3.0 * rho)
    proj = [
        xx * sh[0] + xy * sh[1] + xz * sh[2],
        xy * sh[0] + yy * sh[1] + yz * sh[2],
        xz * sh[0] + yz * sh[1] + zz * sh[2],
    ]
    heat = [0.5 * (s[10 + i] - 2.0 * proj[i] - sh[i] * trace + 2.0 * rho * norm * sh[i]) for i in range(3)]
    stress = [
        xx - rho * sh[0] * sh[0],
        yy - rho * sh[1] * sh[1],
        zz - rho * sh[2] * sh[2],
        xy - rho * sh[0] * sh[1],
        xz - rho * sh[0] * sh[2],
        yz - rho * sh[1] * sh[2],
    ]
    return [rho] + mean + [temp] + stress + heat


def moments_first(part_ref):
    every = part_ref[...].reshape(NVEL, 4, 4, LANES)
    lane = lane_iota((NVEL, LANES)) // CELL
    q = [None] * 16
    for r in range(4):
        blocks = [every[:, b, r, :] for b in range(4)]
        for g in range(4):
            row = jnp.zeros((NVEL, LANES), jnp.float32)
            for b in range(4):
                shift = CELL * ((b - g) % 4)
                row = jnp.where(lane == b, pltpu.roll(blocks[b], shift, 1) if shift else blocks[b], row)
            q[4 * g + r] = row
    rho_d, m, s, heat, cen = q[0], q[1:4], q[4:10], q[10:13], q[13:16]
    rho = rows_sum(rho_d)
    u = [rows_sum(m[i] + rho_d * cen[i]) / rho for i in range(3)]
    d = [cen[i] - u[i] for i in range(3)]
    tensor = ((0, 3, 4), (3, 1, 5), (4, 5, 2))
    pairs = ((0, 0), (1, 1), (2, 2), (0, 1), (0, 2), (1, 2))
    d2 = d[0] * d[0] + d[1] * d[1] + d[2] * d[2]
    m_d = m[0] * d[0] + m[1] * d[1] + m[2] * d[2]
    total = s[0] + s[1] + s[2] + 2.0 * m_d + rho_d * d2
    sums = [rho] + [rows_sum(m[i] + rho_d * d[i]) for i in range(3)]
    for n, (i, j) in enumerate(pairs):
        sums.append(rows_sum(s[n] + m[i] * d[j] + d[i] * m[j] + rho_d * d[i] * d[j]))
    for i in range(3):
        along = s[tensor[i][0]] * d[0] + s[tensor[i][1]] * d[1] + s[tensor[i][2]] * d[2]
        sums.append(rows_sum(heat[i] + 2.0 * along + m[i] * d2 + d[i] * total))
    return finish_rows(rho, u, sums)


def moments_next(part_ref, cen_ref):
    total = part_ref[0]
    for n in range(1, NVEL):
        total = total + part_ref[n]
    s = [total[i : i + 1] for i in range(13)]
    return finish_rows(s[0], [cen_ref[i : i + 1] for i in range(3)], s)


def relax(sc, moments, num_ref, out_ref, par_ref, f_out, part_ref, cen_ref, tabs):
    zt_ref, zq_ref, zg_ref, cz_ref, f_ref, sems = tabs
    size = CHUNK // PIECES
    moments = moments()
    plane, first_b = sc[3], sc[4]
    rho, ux, uy, uz, temp = moments[0:5]
    heat = moments[11:14]
    vol = par_ref[R_VOL : R_VOL + 1]
    log_t = jnp.log(temp)
    rate = rho * jnp.exp((1.0 - VISC_EXPONENT) * log_t) * (1.0 / MU_REF)
    volrate = vol * rate
    fixed = vol / TIME_STEP + volrate
    scale = volrate * rho * jnp.exp(-1.5 * log_t)
    inv_t = 1.0 / temp
    mult = (1.0 - DIFFUSIVITY_RAT) / (5.0 * rho * temp * temp)
    heat = [mult * h for h in heat]
    cx = place(jnp.full((1, LANES), plane, jnp.int32)) - ux
    cx2 = cx * cx
    cz = place(row_iota((NC, LANES))) - uz
    cz_ref[...] = cz
    zt = cz * cz * inv_t
    zt_ref[...] = zt
    zg_ref[...] = jnp.exp(-0.5 * zt)
    zq_ref[...] = cz * heat[2]
    x_t = cx2 * inv_t
    x_q = cx * heat[0]
    zero = jnp.zeros((8, LANES), jnp.float32)

    unroll = 4

    def body(step, acc):
        acc = list(acc)
        for part in range(unroll):
            b = step * unroll + part
            cy = place(jnp.full((1, LANES), first_b + b, jnp.int32)) - uy
            cy2 = cy * cy
            xy_t = x_t + cy2 * inv_t
            xy_g = scale * jnp.exp(-0.5 * xy_t)
            xy_t = xy_t - 5.0
            xy_q = x_q + cy * heat[1]
            p = [None] * 4
            for ct in range(NC // 8):
                loc = slice(ct * 8, ct * 8 + 8)
                rows = pl.ds(pl.multiple_of(b * NC + ct * 8, 8), 8)
                poly = 1.0 + (xy_q + zq_ref[loc]) * (xy_t + zt_ref[loc])
                num = num_ref[rows, :] + (xy_g * zg_ref[loc]) * poly
                den = fixed + out_ref[rows, :]
                f = num / den
                f_ref[rows, :] = f
                c = cz_ref[loc]
                for power in range(4):
                    p[power] = f if p[power] is None else p[power] + f
                    if power < 3:
                        f = f * c
            new = [
                p[0], cy * p[0], cy2 * p[0], cy2 * cy * p[0],
                p[1], cy * p[1], cy2 * p[1],
                p[2], cy * p[2],
                p[3],
            ]
            acc = [o + n for o, n in zip(acc, new)]
        return tuple(acc)

    acc = (zero,) * 10
    sends = []
    steps = NB // unroll // PIECES
    for piece in range(PIECES):
        acc = lax.fori_loop(piece * steps, (piece + 1) * steps, body, acc)
        if f_out is not None:
            rows = pl.ds(piece * size, size)
            sends += start_all([(f_ref.at[rows], f_out.at[rows])], sems.at[pl.ds(piece, 1)])
    t0, t0y, t0yy, t0yyy, t1, t1y, t1yy, t2, t2y, t3 = [rows_sum(a) * WEIGHT for a in acc]
    rows = [
        t0, cx * t0, t0y, t1,
        cx2 * t0, t0yy, t2, cx * t0y, cx * t1, t1y,
        cx * (cx2 * t0 + t0yy + t2),
        cx2 * t0y + t0yyy + t2y,
        cx2 * t1 + t1yy + t3,
    ]
    for i, row in enumerate(rows):
        part_ref[i : i + 1] = row
    part_ref[13:16] = jnp.zeros((3, LANES), jnp.float32)
    for i, row in enumerate((ux, uy, uz)):
        cen_ref[i : i + 1] = row
    cen_ref[3:8] = jnp.zeros((5, LANES), jnp.float32)
    wait_all(sends)


def relax_first_kernel(sc, parts, num, out, par_ref, f_out, part_ref, cen_ref, *tabs):
    relax(sc, lambda: moments_first(parts), num, out, par_ref, f_out, part_ref, cen_ref, tabs)


def relax_next_kernel(sc, parts, num, out, par_ref, old_ref, f_out, part_ref, cen_ref, *tabs):
    relax(sc, lambda: moments_next(parts, old_ref), num, out, par_ref, f_out, part_ref, cen_ref, tabs)


def relax_last_kernel(sc, parts, num, out, par_ref, old_ref, o0, o1, o2, o3, copies, cen_ref, *scratch):
    tabs, (stack, part_ref) = scratch[0:6], scratch[6:8]
    f_ref = tabs[4]
    y = sc[0]
    relax(sc, lambda: moments_next(parts, old_ref), num, out, par_ref, None, part_ref, cen_ref, tabs)
    for blk in range(CHUNK // LANES):
        cols = slice(blk * LANES, (blk + 1) * LANES)
        stack[:, cols] = f_ref[cols, :].T
    for k, o in enumerate((o0, o1, o2, o3)):
        row = pl.multiple_of((y ^ k) * CELL, 8)
        o[...] = stack[pl.ds(row, CELL), :]
    part = part_ref[...]
    for n in range(NVEL):
        copies[n] = part


def sum_kernel(p0, p1, p2, p3, out):
    total = (p0[...] + p1[...]) + (p2[...] + p3[...])
    for n in range(NVEL):
        out[n] = total


def total_kernel(sc, parts, p0, p1, p2, p3):
    total = functools.reduce(jnp.add, [parts[n] for n in range(NVEL)])
    total = pltpu.roll(total, (LANES - sc[0] * CELL) % LANES, 1)
    y = sc[0]
    for k, out in enumerate((p0, p1, p2, p3)):
        out[...] = pack(pltpu.roll(total, (4 + y - (y ^ k)) % 4 * CELL, 1), 0)


def end_kernel(sc, t0, t1, t2, t3, cen_ref, r0, r1, r2, r3, out, table_ref, sems):
    y = sc[0]
    pairs = []
    for k, r in enumerate((r0, r1, r2, r3)):
        pairs.append((r, out.at[:, pl.ds(pl.multiple_of((y ^ k) * CHUNK, LANES), CHUNK)]))
    sends = start_all(pairs, sems)
    total = (t0[...] + t1[...]) + (t2[...] + t3[...])
    cen = pltpu.roll(cen_ref[...], (LANES - y * CELL) % LANES, 1)
    sums = [None] * 16
    for g in range(4):
        rows = pltpu.roll(total, LANES - CELL * g, 1) if g else total
        for r in range(4):
            sums[4 * g + r] = rows[r : r + 1]
    rows = finish_rows(sums[0], [cen[i : i + 1] for i in range(3)], sums)
    for i, row in enumerate(rows):
        table_ref[i : i + 1] = row[:, 0:CELL]
    wait_all(sends)


def call(kernel, name, spaces, out_shapes, scratch=(), scalars=True, limit=VMEM_LIMIT):
    spec = {"v": pl.BlockSpec(memory_space=pltpu.VMEM)}
    spec["o"] = spec["v"]
    spec["a"] = spec["h"] = pl.BlockSpec(memory_space=pl.ANY)
    spaces, out_spaces = spaces.split()
    place_out = {"v": pltpu.VMEM, "h": pltpu.HBM, "o": jax.ShapeDtypeStruct}
    shapes = tuple(place_out[space](o.shape, o.dtype) for space, o in zip(out_spaces, out_shapes))
    specs = tuple(spec[space] for space in out_spaces)
    kernel_call = pl.pallas_call(
        kernel,
        name=name,
        out_shape=shapes,
        in_specs=[pl.BlockSpec(memory_space=pltpu.SMEM)] * scalars + [spec[space] for space in spaces],
        out_specs=specs,
        scratch_shapes=list(scratch),
        compiler_params=pltpu.CompilerParams(vmem_limit_bytes=limit),
        cost_estimate=pl.CostEstimate(flops=1000, bytes_accessed=1000, transcendentals=0),
    )

    def run(*args):
        first = len(args) - len(spaces)
        placed = [
            pltpu.with_memory_space_constraint(x, pltpu.HBM) if space == "h" else x
            for space, x in zip(spaces, args[first:])
        ]
        return kernel_call(*args[:first], *placed)

    return run


def f32(*shape):
    return jax.ShapeDtypeStruct(shape, jnp.float32)


def toward_y(values):
    out = [values[0]]
    for k in (1, 3, 2):
        out.append(lax.ppermute(values[k], "y", [(m, m ^ k) for m in range(4)]))
    return [out[0], out[1], out[3], out[2]]


def other_core(value):
    return lax.ppermute(value, "core", [(0, 1), (1, 0)])


def spread(copies):
    return lax.all_to_all(copies, ("z", "x"), 0, 0)


def exchange(packed):
    return lax.all_to_all(packed, ("z", "x", "y"), 0, 0)


def summed(part, f):
    copies = call(sum_kernel, "copies", "vvvv v", (f32(NVEL, 16, LANES),), scalars=False, limit=SMALL_LIMIT)
    g = other_core(f)
    arrived = toward_y([part] * 4)
    return spread(copies(*arrived)[0]), g


def local(dist_old, volume, area, normals, neighbor, union_rows, union_index):
    vel = lax.axis_index("z") * 4 + lax.axis_index("x")
    y, core = lax.axis_index("y"), lax.axis_index("core")
    sc = jnp.stack([y, core, vel, 2 * vel + y // 2, NB * (y % 2)]).astype(jnp.int32)
    mine = lax.dynamic_index_in_dim(union_index.reshape(8, 4, 2, 8), core, 2, keepdims=False)
    slots = jnp.repeat(jnp.transpose(mine, (0, 2, 1)).reshape(64, 4), CELL, axis=1)

    *pays, packed = call(
        first_kernel,
        "first",
        "haaaaa vvvvo",
        (f32(CELL, PAY),) * 4 + (f32(NSRC, 4, LANES),),
        (
            pltpu.VMEM((CELL, VEL), jnp.float32),
            pltpu.VMEM((R_PAR, LANES), jnp.float32),
            pltpu.SemaphoreType.DMA((9,)),
            pltpu.VMEM((FACES, CELL), jnp.float32),
            pltpu.VMEM((3, FACES, CELL), jnp.float32),
            pltpu.VMEM((1, CELL), jnp.float32),
            pltpu.VMEM((FACES, CELL), jnp.int32),
            pltpu.VMEM((1, 16), jnp.int32),
        ),
    )(sc, dist_old, area, normals, volume[None], neighbor, union_rows)
    got = toward_y(pays)
    peers = [other_core(g) for g in got]
    parts = exchange(packed)
    state = f32(CHUNK, LANES)
    big = pltpu.VMEM((CHUNK, LANES), jnp.float32)
    hots = pltpu.VMEM((2 * LANES, FACES * LANES), jnp.bfloat16)
    ztab = (pltpu.VMEM((FACES, NC, LANES), jnp.float32),)
    base, outflow, num, hot, par = call(
        prepare_kernel,
        "prepare",
        "ahhhhhhhv hvvhv",
        (state, state, state, jax.ShapeDtypeStruct((2 * LANES, FACES * LANES), jnp.bfloat16), f32(R_PAR, LANES)),
        (
            pltpu.VMEM((LANES, PAY), jnp.float32),
            pltpu.VMEM((LANES, PAY), jnp.float32),
            big,
            big,
        )
        + ztab
        + (pltpu.VMEM((NC, LANES), jnp.float32), pltpu.SemaphoreType.DMA((8,)), big, hots),
    )(sc, *got, *peers, slots)
    tabs = (pltpu.VMEM((NC, LANES), jnp.float32),) * 4 + (big, pltpu.SemaphoreType.DMA((PIECES,)))
    faces_next = call(
        faces_kernel, "faces", "aahhv v", (state,), ztab + (big, big, big, hots, pltpu.SemaphoreType.DMA((4,)))
    )
    small = (f32(16, LANES), f32(8, LANES))

    f, part, cen = call(relax_first_kernel, "relax_first", "vvvv vvv", (state,) + small, tabs)(
        sc, parts, num, outflow, par
    )
    relax_next = call(relax_next_kernel, "relax_next", "vvvvv vvv", (state,) + small, tabs)
    parts, g = summed(part, f)
    (num,) = faces_next(sc, f, g, base, hot, par)
    f, part, cen = relax_next(sc, parts, num, outflow, par, cen)
    parts, g = summed(part, f)
    (num,) = faces_next(sc, f, g, base, hot, par)
    *chunks, copies, cen = call(
        relax_last_kernel,
        "relax_last",
        "vvvvv vvvvov",
        (f32(CELL, CHUNK),) * 4 + (f32(NVEL, 16, LANES), f32(8, LANES)),
        tabs
        + (
            pltpu.VMEM((LANES, CHUNK), jnp.float32),
            pltpu.VMEM((16, LANES), jnp.float32),
        ),
    )(sc, parts, num, outflow, par, cen)
    parts = spread(copies)
    blocks = toward_y(chunks)
    packs = call(total_kernel, "total", "v vvvv", (f32(4, LANES),) * 4, limit=SMALL_LIMIT)(sc, parts)
    totals = toward_y(packs)
    end = call(
        end_kernel, "end", "vvvvvaaaa ho", (f32(CELL, VEL), f32(14, CELL)), (pltpu.SemaphoreType.DMA((4,)),)
    )
    return tuple(end(sc, *totals, cen, *blocks))


def solution(mesh):
    cells, vels = ("y", "core"), ("z", "x")
    placed = (
        P(cells, vels),
        P(cells),
        P(None, cells),
        P(None, None, cells),
        P(None, cells),
        P(cells, None),
        P(),
    )
    return jax.shard_map(
        local,
        mesh=jax.sharding.Mesh(mesh.devices.reshape(8, 4, 4, 2), ("z", "x", "y", "core")),
        in_specs=placed,
        out_specs=(P(cells, vels), P(None, cells)),
        check_vma=False,
    )
```

```python
import functools
import math

import jax
import jax.numpy as jnp
from jax import lax
from jax.experimental import pallas as pl
from jax.experimental.pallas import tpu as pltpu
from jax.sharding import PartitionSpec as P

VGRID = 64
SPEED_LIMIT = 10.0
TIME_STEP = 0.5
MU_REF = 0.5
VISC_EXPONENT = 0.81
DIFFUSIVITY_RAT = 2.0 / 3.0
INFLOW_SPEED = 5.0
H = 2.0 * SPEED_LIMIT / VGRID
WEIGHT = H**3 / (2.0 * math.pi) ** 1.5

CELL = 32
FACES = 4
LANES = 128
CHUNK = 2048
VEL = 8192
NB = 32
NC = 64
NVEL = 32
PIECES = 4
PAY = CHUNK + LANES
NSRC = 4 * NVEL
VMEM_LIMIT = 12 * 1024 * 1024
SMALL_LIMIT = 4 * 1024 * 1024

R_AREA, R_NORM, R_VOL, R_NEIGH, R_UNION, R_PAR = 0, 4, 16, 17, 21, 24


def place(level):
    return (level.astype(jnp.float32) + 0.5) * H - SPEED_LIMIT


def lane_iota(shape):
    return lax.broadcasted_iota(jnp.int32, shape, 1)


def row_iota(shape):
    return lax.broadcasted_iota(jnp.int32, shape, 0)


def rows_sum(x):
    return jnp.sum(x, axis=0, keepdims=True)


def pack(part, block):
    lane = lane_iota((4, LANES)) // CELL
    out = jnp.zeros((4, LANES), jnp.float32)
    for g in range(4):
        shift = CELL * ((g - block) % 4)
        rows = part[4 * g : 4 * g + 4]
        out = jnp.where(lane == g, pltpu.roll(rows, shift, 1) if shift else rows, out)
    return out


def first_kernel(sc, dist, area, normals, volume, neighbor, union, *refs):
    outs, packed, (d_ref, par_ref, sems), small = refs[0:4], refs[4], refs[5:8], refs[8:13]
    pairs = list(zip((area, normals, volume, neighbor, union), small))
    params = [pltpu.make_async_copy(a, b, sems.at[4 + i]) for i, (a, b) in enumerate(pairs)]
    for copy in params:
        copy.start()
    copies = []
    for group in range(4):
        rows = pl.ds(8 * group, 8)
        copies.append(pltpu.make_async_copy(dist.at[rows], d_ref.at[rows], sems.at[group]))
        copies[-1].start()
    y = sc[0]
    vel = sc[2]
    par_ref[...] = jnp.zeros((R_PAR, LANES), jnp.float32)
    for copy in params:
        copy.wait()
    area, normals, volume, neighbor, union = small
    par_ref[R_AREA : R_AREA + FACES, 0:CELL] = area[...]
    for d in range(3):
        par_ref[R_NORM + FACES * d : R_NORM + FACES * (d + 1), 0:CELL] = normals[d]
    par_ref[R_VOL : R_VOL + 1, 0:CELL] = volume[...]
    par_ref[R_NEIGH : R_NEIGH + FACES, 0:CELL] = neighbor[...].astype(jnp.float32)
    par_ref[R_UNION : R_UNION + 1, 0:16] = union[...].astype(jnp.float32)
    par = pltpu.roll(par_ref[...], y * CELL, 1)
    for out in outs:
        out[0:R_PAR, CHUNK:PAY] = par
        out[R_PAR:CELL, CHUNK:PAY] = jnp.zeros((CELL - R_PAR, LANES), jnp.float32)
    lane = lane_iota((8, LANES))
    par_y = (lane // NC).astype(jnp.float32) * H
    vz = place(lane % NC)
    base_y = par_y + (0.5 * H - SPEED_LIMIT)
    vx = [place(jnp.full((8, LANES), 2 * vel + a, jnp.int32)) for a in range(2)]
    wait_all(copies)
    centers = []
    for group in range(4):
        rows = slice(8 * group, 8 * group + 8)
        a0 = [None, None]
        a1 = None
        for a in range(2):
            for t in range(32):
                x = d_ref[rows, pl.ds((a * 32 + t) * LANES, LANES)]
                a0[a] = x if t == 0 else a0[a] + x
                if t:
                    a1 = x * float(t) if a1 is None else a1 + x * float(t)
        both = a0[0] + a0[1]
        totals = [both, a0[0] * vx[0] + a0[1] * vx[1], a1 * (2.0 * H) + both * base_y, both * vz]
        rho, *first = [jnp.sum(total, axis=1, keepdims=True) for total in totals]
        inv = 1.0 / jnp.maximum(rho, 1e-30)
        centers.append([jnp.clip(total * inv, -SPEED_LIMIT, SPEED_LIMIT) for total in first])
    tiles = []
    for group in range(4):
        rows = slice(8 * group, 8 * group + 8)
        cen_x, cen_y, cen_z = centers[group]
        cz = vz - cen_z
        cz2 = cz * cz
        start_y = base_y - cen_y
        sums = [None] * 13

        def add(index, value):
            sums[index] = value if sums[index] is None else sums[index] + value

        for a in range(2):
            p = [None] * 4
            for t in range(32):
                x = d_ref[rows, pl.ds((a * 32 + t) * LANES, LANES)]
                cy = start_y + 2.0 * H * t
                for power in range(4):
                    p[power] = x if t == 0 else p[power] + x
                    if power < 3:
                        x = x * cy
            cx = vx[a] - cen_x
            cx2 = cx * cx
            xz0 = (cx2 + cz2) * p[0] + p[2]
            add(0, p[0])
            add(1, cx * p[0])
            add(2, p[1])
            add(3, cz * p[0])
            add(4, cx2 * p[0])
            add(5, p[2])
            add(6, cz2 * p[0])
            add(7, cx * p[1])
            add(8, cx * cz * p[0])
            add(9, cz * p[1])
            add(10, cx * xz0)
            add(11, (cx2 + cz2) * p[1] + p[3])
            add(12, cz * xz0)
        cols = [jnp.sum(s, axis=1, keepdims=True) * WEIGHT for s in sums]
        cols += [cen_x, cen_y, cen_z]
        tile = jnp.zeros((8, LANES), jnp.float32)
        for q, col in enumerate(cols):
            tile = jnp.where(lane == q, col, tile)
        tiles.append(tile)
    for k, out in enumerate(outs):
        chunk = pl.multiple_of((y ^ k) * CHUNK, LANES)
        out[:, 0:CHUNK] = d_ref[:, pl.ds(chunk, CHUNK)]
    square = jnp.concatenate(tiles + [jnp.zeros((LANES - CELL, LANES), jnp.float32)], 0)
    block = pack(square.T[0:16], 0)
    for n in range(NSRC):
        packed[n] = block


def face_tables(par, vz):
    scaled = []
    for j in range(FACES):
        area = par[R_AREA + j : R_AREA + j + 1]
        n = [par[R_NORM + 4 * d + j : R_NORM + 4 * d + j + 1] * area for d in range(3)]
        scaled.append(n)
    return scaled


def start_all(pairs, sems):
    copies = [pltpu.make_async_copy(a, b, sems.at[i]) for i, (a, b) in enumerate(pairs)]
    for copy in copies:
        copy.start()
    return copies


def wait_all(copies):
    for copy in copies:
        copy.wait()


def to_lanes(stack, out):
    for blk in range(CHUNK // LANES):
        cols = slice(blk * LANES, (blk + 1) * LANES)
        out[cols, :] = stack[:, cols].T


def params_of(blocks):
    return functools.reduce(jnp.add, [blocks[n * CELL : n * CELL + R_PAR, CHUNK : CHUNK + LANES] for n in range(4)])


def prepare_kernel(sc, p0, p1, p2, p3, q0, q1, q2, q3, ui_ref, base, out_ref, num_ref, hot, par_ref, *scratch):
    pays, peers, dt_ref, gt_ref, ztab, ftab, sems, base_ref, hot_ref = scratch
    y, plane, first_b = sc[0], sc[3], sc[4]
    pairs = []
    for stack, blocks in ((pays, (p0, p1, p2, p3)), (peers, (q0, q1, q2, q3))):
        for k, block in enumerate(blocks):
            row = pl.multiple_of((y ^ k) * CELL, 8)
            pairs.append((block, stack.at[pl.ds(row, CELL)]))
    wait_all(start_all(pairs, sems))
    par = params_of(pays)
    par_ref[...] = par
    to_lanes(pays, dt_ref)
    to_lanes(peers, gt_ref)
    gather_table(sc, par, params_of(peers)[R_UNION : R_UNION + 1], ui_ref, hot_ref)
    masks = [(par[R_NEIGH + j : R_NEIGH + j + 1] >= CELL + 64 - 0.5).astype(jnp.float32) for j in range(FACES)]
    vz = place(row_iota((NC, LANES)))
    scaled = face_tables(par, vz)
    for j in range(FACES):
        ztab[j] = scaled[j][2] * vz
    ftab[...] = jnp.exp(-0.5 * vz * vz)
    vx = place(jnp.full((1, LANES), plane, jnp.int32))
    stay = par[R_VOL : R_VOL + 1] / TIME_STEP

    def body(b, _):
        vy = place(jnp.full((1, LANES), first_b + b, jnp.int32))
        free = jnp.exp(-0.5 * ((vx - INFLOW_SPEED) ** 2 + vy * vy))
        xy = [scaled[j][0] * vx + scaled[j][1] * vy for j in range(FACES)]
        for ct in range(NC // 8):
            rows = pl.ds(pl.multiple_of(b * NC + ct * 8, 8), 8)
            outflow = jnp.zeros((8, LANES), jnp.float32)
            inflow = jnp.zeros((8, LANES), jnp.float32)
            for j in range(FACES):
                s = xy[j] + ztab[j, ct * 8 : ct * 8 + 8]
                outflow = outflow + jnp.maximum(s, 0.0)
                inflow = inflow + jnp.maximum(-s, 0.0) * masks[j]
            out_ref[rows, :] = outflow
            base_ref[rows, :] = stay * dt_ref[rows, :] + (free * ftab[ct * 8 : ct * 8 + 8]) * inflow
        return 0

    lax.fori_loop(0, NB, body, 0)
    sends = start_all(((base_ref, base), (hot_ref, hot)), sems)
    faces(sc, dt_ref, gt_ref, base_ref, hot_ref, par_ref, num_ref, ztab)
    wait_all(sends)


def gather_table(sc, par, peer, ui_ref, hot_ref):
    core = sc[1]
    lane = lane_iota((1, LANES))
    own_rows = jnp.broadcast_to(par[R_UNION : R_UNION + 1], (LANES, LANES)).T
    peer_rows = jnp.broadcast_to(peer, (LANES, LANES)).T
    slots = row_iota((64, LANES))
    entries = row_iota((LANES, LANES))
    for j in range(FACES):
        e = par[R_NEIGH + j : R_NEIGH + j + 1].astype(jnp.int32)
        off = jnp.clip(e - CELL, 0, 63)
        source = off // 8
        position = rows_sum(jnp.where(slots == off, ui_ref[...], 0))
        entry = (source // 2) * CELL + position
        mine = (source % 2) == core
        found = jnp.where(entries == entry, jnp.where(mine, own_rows, peer_rows), 0.0)
        remote = rows_sum(found).astype(jnp.int32) + (source // 2) * CELL + jnp.where(mine, 0, LANES)
        local_row = (lane // CELL) * CELL + e
        target = jnp.where(e < CELL, local_row, jnp.where(e < CELL + 64, remote, -1))
        hot = (row_iota((2 * LANES, LANES)) == target).astype(jnp.float32)
        hot_ref[:, j * LANES : (j + 1) * LANES] = hot.astype(jnp.bfloat16)


def faces_kernel(sc, f, g, base, hot, par_ref, num_ref, ztab, f_ref, g_ref, base_ref, hot_ref, sems):
    wait_all(start_all(((f, f_ref), (g, g_ref), (base, base_ref), (hot, hot_ref)), sems))
    faces(sc, f_ref, g_ref, base_ref, hot_ref, par_ref, num_ref, ztab)


def faces(sc, f_ref, g_ref, base_ref, hot_ref, par_ref, num_ref, ztab):
    plane, first_b = sc[3], sc[4]
    par = par_ref[...]
    vz = place(row_iota((NC, LANES)))
    scaled = face_tables(par, vz)
    for j in range(FACES):
        ztab[j] = scaled[j][2] * vz
    vx = place(jnp.full((1, LANES), plane, jnp.int32))
    step_b = 8
    size = step_b * NC
    hot = jnp.concatenate([hot_ref[...]] * 2, 0)

    def body(it, _):
        rows = pl.ds(pl.multiple_of(it * size, size), size)
        x = jnp.concatenate([f_ref[rows, :], g_ref[rows, :]], 1)
        high = x.astype(jnp.bfloat16)
        low = (x - high.astype(jnp.float32)).astype(jnp.bfloat16)
        got = jnp.dot(jnp.concatenate([high, low], 1), hot, preferred_element_type=jnp.float32)
        for bb in range(step_b):
            vy = place(jnp.full((1, LANES), first_b + it * step_b + bb, jnp.int32))
            total = base_ref[pl.ds(pl.multiple_of(it * size + bb * NC, NC), NC), :]
            for j in range(FACES):
                xy = scaled[j][0] * vx + scaled[j][1] * vy
                s = xy + ztab[j]
                total = total - jnp.minimum(s, 0.0) * got[bb * NC : (bb + 1) * NC, j * LANES : (j + 1) * LANES]
            num_ref[pl.ds(pl.multiple_of(it * size + bb * NC, NC), NC), :] = total
        return 0

    lax.fori_loop(0, NB // step_b, body, 0)


def finish_rows(rho, center, s):
    sh = [s[i] / rho for i in (1, 2, 3)]
    mean = [center[i] + sh[i] for i in range(3)]
    xx, yy, zz, xy, xz, yz = s[4:10]
    trace = xx + yy + zz
    norm = sh[0] * sh[0] + sh[1] * sh[1] + sh[2] * sh[2]
    temp = (trace - rho * norm) / (3.0 * rho)
    proj = [
        xx * sh[0] + xy * sh[1] + xz * sh[2],
        xy * sh[0] + yy * sh[1] + yz * sh[2],
        xz * sh[0] + yz * sh[1] + zz * sh[2],
    ]
    heat = [0.5 * (s[10 + i] - 2.0 * proj[i] - sh[i] * trace + 2.0 * rho * norm * sh[i]) for i in range(3)]
    stress = [
        xx - rho * sh[0] * sh[0],
        yy - rho * sh[1] * sh[1],
        zz - rho * sh[2] * sh[2],
        xy - rho * sh[0] * sh[1],
        xz - rho * sh[0] * sh[2],
        yz - rho * sh[1] * sh[2],
    ]
    return [rho] + mean + [temp] + stress + heat


def moments_first(part_ref):
    every = part_ref[...].reshape(NVEL, 4, 4, LANES)
    lane = lane_iota((NVEL, LANES)) // CELL
    q = [None] * 16
    for r in range(4):
        blocks = [every[:, b, r, :] for b in range(4)]
        for g in range(4):
            row = jnp.zeros((NVEL, LANES), jnp.float32)
            for b in range(4):
                shift = CELL * ((b - g) % 4)
                row = jnp.where(lane == b, pltpu.roll(blocks[b], shift, 1) if shift else blocks[b], row)
            q[4 * g + r] = row
    rho_d, m, s, heat, cen = q[0], q[1:4], q[4:10], q[10:13], q[13:16]
    rho = rows_sum(rho_d)
    u = [rows_sum(m[i] + rho_d * cen[i]) / rho for i in range(3)]
    d = [cen[i] - u[i] for i in range(3)]
    tensor = ((0, 3, 4), (3, 1, 5), (4, 5, 2))
    pairs = ((0, 0), (1, 1), (2, 2), (0, 1), (0, 2), (1, 2))
    d2 = d[0] * d[0] + d[1] * d[1] + d[2] * d[2]
    m_d = m[0] * d[0] + m[1] * d[1] + m[2] * d[2]
    total = s[0] + s[1] + s[2] + 2.0 * m_d + rho_d * d2
    sums = [rho] + [rows_sum(m[i] + rho_d * d[i]) for i in range(3)]
    for n, (i, j) in enumerate(pairs):
        sums.append(rows_sum(s[n] + m[i] * d[j] + d[i] * m[j] + rho_d * d[i] * d[j]))
    for i in range(3):
        along = s[tensor[i][0]] * d[0] + s[tensor[i][1]] * d[1] + s[tensor[i][2]] * d[2]
        sums.append(rows_sum(heat[i] + 2.0 * along + m[i] * d2 + d[i] * total))
    return finish_rows(rho, u, sums)


def moments_next(part_ref, cen_ref):
    total = part_ref[0]
    for n in range(1, NVEL):
        total = total + part_ref[n]
    s = [total[i : i + 1] for i in range(13)]
    return finish_rows(s[0], [cen_ref[i : i + 1] for i in range(3)], s)


def relax(sc, moments, num_ref, out_ref, par_ref, f_out, part_ref, cen_ref, tabs):
    zt_ref, zq_ref, zg_ref, cz_ref, f_ref, sems = tabs
    size = CHUNK // PIECES
    moments = moments()
    plane, first_b = sc[3], sc[4]
    rho, ux, uy, uz, temp = moments[0:5]
    heat = moments[11:14]
    vol = par_ref[R_VOL : R_VOL + 1]
    log_t = jnp.log(temp)
    rate = rho * jnp.exp((1.0 - VISC_EXPONENT) * log_t) * (1.0 / MU_REF)
    volrate = vol * rate
    fixed = vol / TIME_STEP + volrate
    scale = volrate * rho * jnp.exp(-1.5 * log_t)
    inv_t = 1.0 / temp
    mult = (1.0 - DIFFUSIVITY_RAT) / (5.0 * rho * temp * temp)
    heat = [mult * h for h in heat]
    cx = place(jnp.full((1, LANES), plane, jnp.int32)) - ux
    cx2 = cx * cx
    cz = place(row_iota((NC, LANES))) - uz
    cz_ref[...] = cz
    zt = cz * cz * inv_t
    zt_ref[...] = zt
    zg_ref[...] = jnp.exp(-0.5 * zt)
    zq_ref[...] = cz * heat[2]
    x_t = cx2 * inv_t
    x_q = cx * heat[0]
    zero = jnp.zeros((8, LANES), jnp.float32)

    unroll = 4

    def body(step, acc):
        acc = list(acc)
        for part in range(unroll):
            b = step * unroll + part
            cy = place(jnp.full((1, LANES), first_b + b, jnp.int32)) - uy
            cy2 = cy * cy
            xy_t = x_t + cy2 * inv_t
            xy_g = scale * jnp.exp(-0.5 * xy_t)
            xy_t = xy_t - 5.0
            xy_q = x_q + cy * heat[1]
            p = [None] * 4
            for ct in range(NC // 8):
                loc = slice(ct * 8, ct * 8 + 8)
                rows = pl.ds(pl.multiple_of(b * NC + ct * 8, 8), 8)
                poly = 1.0 + (xy_q + zq_ref[loc]) * (xy_t + zt_ref[loc])
                num = num_ref[rows, :] + (xy_g * zg_ref[loc]) * poly
                den = fixed + out_ref[rows, :]
                f = num / den
                f_ref[rows, :] = f
                c = cz_ref[loc]
                for power in range(4):
                    p[power] = f if p[power] is None else p[power] + f
                    if power < 3:
                        f = f * c
            new = [
                p[0], cy * p[0], cy2 * p[0], cy2 * cy * p[0],
                p[1], cy * p[1], cy2 * p[1],
                p[2], cy * p[2],
                p[3],
            ]
            acc = [o + n for o, n in zip(acc, new)]
        return tuple(acc)

    acc = (zero,) * 10
    sends = []
    steps = NB // unroll // PIECES
    for piece in range(PIECES):
        acc = lax.fori_loop(piece * steps, (piece + 1) * steps, body, acc)
        if f_out is not None:
            rows = pl.ds(piece * size, size)
            sends += start_all([(f_ref.at[rows], f_out.at[rows])], sems.at[pl.ds(piece, 1)])
    t0, t0y, t0yy, t0yyy, t1, t1y, t1yy, t2, t2y, t3 = [rows_sum(a) * WEIGHT for a in acc]
    rows = [
        t0, cx * t0, t0y, t1,
        cx2 * t0, t0yy, t2, cx * t0y, cx * t1, t1y,
        cx * (cx2 * t0 + t0yy + t2),
        cx2 * t0y + t0yyy + t2y,
        cx2 * t1 + t1yy + t3,
    ]
    for i, row in enumerate(rows):
        part_ref[i : i + 1] = row
    part_ref[13:16] = jnp.zeros((3, LANES), jnp.float32)
    for i, row in enumerate((ux, uy, uz)):
        cen_ref[i : i + 1] = row
    cen_ref[3:8] = jnp.zeros((5, LANES), jnp.float32)
    wait_all(sends)


def relax_first_kernel(sc, parts, num, out, par_ref, f_out, part_ref, cen_ref, *tabs):
    relax(sc, lambda: moments_first(parts), num, out, par_ref, f_out, part_ref, cen_ref, tabs)


def relax_next_kernel(sc, parts, num, out, par_ref, old_ref, f_out, part_ref, cen_ref, *tabs):
    relax(sc, lambda: moments_next(parts, old_ref), num, out, par_ref, f_out, part_ref, cen_ref, tabs)


def relax_last_kernel(sc, parts, num, out, par_ref, old_ref, o0, o1, o2, o3, copies, cen_ref, *scratch):
    tabs, (stack, part_ref) = scratch[0:6], scratch[6:8]
    f_ref = tabs[4]
    y = sc[0]
    relax(sc, lambda: moments_next(parts, old_ref), num, out, par_ref, None, part_ref, cen_ref, tabs)
    for blk in range(CHUNK // LANES):
        cols = slice(blk * LANES, (blk + 1) * LANES)
        stack[:, cols] = f_ref[cols, :].T
    for k, o in enumerate((o0, o1, o2, o3)):
        row = pl.multiple_of((y ^ k) * CELL, 8)
        o[...] = stack[pl.ds(row, CELL), :]
    part = part_ref[...]
    for n in range(NVEL):
        copies[n] = part


def sum_kernel(p0, p1, p2, p3, out):
    total = (p0[...] + p1[...]) + (p2[...] + p3[...])
    for n in range(NVEL):
        out[n] = total


def total_kernel(sc, parts, p0, p1, p2, p3):
    total = functools.reduce(jnp.add, [parts[n] for n in range(NVEL)])
    total = pltpu.roll(total, (LANES - sc[0] * CELL) % LANES, 1)
    y = sc[0]
    for k, out in enumerate((p0, p1, p2, p3)):
        out[...] = pack(pltpu.roll(total, (4 + y - (y ^ k)) % 4 * CELL, 1), 0)


def assemble_kernel(sc, r0, r1, r2, r3, out, sems):
    pairs = []
    for k, r in enumerate((r0, r1, r2, r3)):
        pairs.append((r, out.at[:, pl.ds(pl.multiple_of((sc[0] ^ k) * CHUNK, LANES), CHUNK)]))
    wait_all(start_all(pairs, sems))


def table_kernel(sc, t0, t1, t2, t3, cen_ref, table_ref):
    total = (t0[...] + t1[...]) + (t2[...] + t3[...])
    cen = pltpu.roll(cen_ref[...], (LANES - sc[0] * CELL) % LANES, 1)
    sums = [None] * 16
    for g in range(4):
        rows = pltpu.roll(total, LANES - CELL * g, 1) if g else total
        for r in range(4):
            sums[4 * g + r] = rows[r : r + 1]
    rows = finish_rows(sums[0], [cen[i : i + 1] for i in range(3)], sums)
    for i, row in enumerate(rows):
        table_ref[i : i + 1] = row[:, 0:CELL]


def call(kernel, name, spaces, out_shapes, scratch=(), scalars=True, limit=VMEM_LIMIT):
    spec = {"v": pl.BlockSpec(memory_space=pltpu.VMEM)}
    spec["o"] = spec["v"]
    spec["a"] = spec["h"] = pl.BlockSpec(memory_space=pl.ANY)
    spaces, out_spaces = spaces.split()
    place_out = {"v": pltpu.VMEM, "h": pltpu.HBM, "o": jax.ShapeDtypeStruct}
    shapes = tuple(place_out[space](o.shape, o.dtype) for space, o in zip(out_spaces, out_shapes))
    specs = tuple(spec[space] for space in out_spaces)
    kernel_call = pl.pallas_call(
        kernel,
        name=name,
        out_shape=shapes,
        in_specs=[pl.BlockSpec(memory_space=pltpu.SMEM)] * scalars + [spec[space] for space in spaces],
        out_specs=specs,
        scratch_shapes=list(scratch),
        compiler_params=pltpu.CompilerParams(vmem_limit_bytes=limit),
        cost_estimate=pl.CostEstimate(flops=1000, bytes_accessed=1000, transcendentals=0),
    )

    def run(*args):
        first = len(args) - len(spaces)
        placed = [
            pltpu.with_memory_space_constraint(x, pltpu.HBM) if space == "h" else x
            for space, x in zip(spaces, args[first:])
        ]
        return kernel_call(*args[:first], *placed)

    return run


def f32(*shape):
    return jax.ShapeDtypeStruct(shape, jnp.float32)


def toward_y(values):
    out = [values[0]]
    for k in (1, 3, 2):
        out.append(lax.ppermute(values[k], "y", [(m, m ^ k) for m in range(4)]))
    return [out[0], out[1], out[3], out[2]]


def other_core(value):
    return lax.ppermute(value, "core", [(0, 1), (1, 0)])


def spread(copies):
    return lax.all_to_all(copies, ("z", "x"), 0, 0)


def exchange(packed):
    return lax.all_to_all(packed, ("z", "x", "y"), 0, 0)


def summed(part, f):
    copies = call(sum_kernel, "copies", "vvvv v", (f32(NVEL, 16, LANES),), scalars=False, limit=SMALL_LIMIT)
    g = other_core(f)
    arrived = toward_y([part] * 4)
    return spread(copies(*arrived)[0]), g


def local(dist_old, volume, area, normals, neighbor, union_rows, union_index):
    vel = lax.axis_index("z") * 4 + lax.axis_index("x")
    y, core = lax.axis_index("y"), lax.axis_index("core")
    sc = jnp.stack([y, core, vel, 2 * vel + y // 2, NB * (y % 2)]).astype(jnp.int32)
    mine = lax.dynamic_index_in_dim(union_index.reshape(8, 4, 2, 8), core, 2, keepdims=False)
    slots = jnp.repeat(jnp.transpose(mine, (0, 2, 1)).reshape(64, 4), CELL, axis=1)

    *pays, packed = call(
        first_kernel,
        "first",
        "hhhhhh vvvvo",
        (f32(CELL, PAY),) * 4 + (f32(NSRC, 4, LANES),),
        (
            pltpu.VMEM((CELL, VEL), jnp.float32),
            pltpu.VMEM((R_PAR, LANES), jnp.float32),
            pltpu.SemaphoreType.DMA((9,)),
            pltpu.VMEM((FACES, CELL), jnp.float32),
            pltpu.VMEM((3, FACES, CELL), jnp.float32),
            pltpu.VMEM((1, CELL), jnp.float32),
            pltpu.VMEM((FACES, CELL), jnp.int32),
            pltpu.VMEM((1, 16), jnp.int32),
        ),
    )(sc, dist_old, area, normals, volume[None], neighbor, union_rows)
    got = toward_y(pays)
    peers = [other_core(g) for g in got]
    parts = exchange(packed)
    state = f32(CHUNK, LANES)
    big = pltpu.VMEM((CHUNK, LANES), jnp.float32)
    hots = pltpu.VMEM((2 * LANES, FACES * LANES), jnp.bfloat16)
    ztab = (pltpu.VMEM((FACES, NC, LANES), jnp.float32),)
    base, outflow, num, hot, par = call(
        prepare_kernel,
        "prepare",
        "ahhhhhhhv hvvhv",
        (state, state, state, jax.ShapeDtypeStruct((2 * LANES, FACES * LANES), jnp.bfloat16), f32(R_PAR, LANES)),
        (
            pltpu.VMEM((LANES, PAY), jnp.float32),
            pltpu.VMEM((LANES, PAY), jnp.float32),
            big,
            big,
        )
        + ztab
        + (pltpu.VMEM((NC, LANES), jnp.float32), pltpu.SemaphoreType.DMA((8,)), big, hots),
    )(sc, *got, *peers, slots)
    tabs = (pltpu.VMEM((NC, LANES), jnp.float32),) * 4 + (big, pltpu.SemaphoreType.DMA((PIECES,)))
    faces_next = call(
        faces_kernel, "faces", "aahhv v", (state,), ztab + (big, big, big, hots, pltpu.SemaphoreType.DMA((4,)))
    )
    small = (f32(16, LANES), f32(8, LANES))

    f, part, cen = call(relax_first_kernel, "relax_first", "vvvv vvv", (state,) + small, tabs)(
        sc, parts, num, outflow, par
    )
    relax_next = call(relax_next_kernel, "relax_next", "vvvvv vvv", (state,) + small, tabs)
    parts, g = summed(part, f)
    (num,) = faces_next(sc, f, g, base, hot, par)
    f, part, cen = relax_next(sc, parts, num, outflow, par, cen)
    parts, g = summed(part, f)
    (num,) = faces_next(sc, f, g, base, hot, par)
    *chunks, copies, cen = call(
        relax_last_kernel,
        "relax_last",
        "vvvvv vvvvov",
        (f32(CELL, CHUNK),) * 4 + (f32(NVEL, 16, LANES), f32(8, LANES)),
        tabs
        + (
            pltpu.VMEM((LANES, CHUNK), jnp.float32),
            pltpu.VMEM((16, LANES), jnp.float32),
        ),
    )(sc, parts, num, outflow, par, cen)
    parts = spread(copies)
    blocks = toward_y(chunks)
    packs = call(total_kernel, "total", "v vvvv", (f32(4, LANES),) * 4, limit=SMALL_LIMIT)(sc, parts)
    totals = toward_y(packs)
    (dist_new,) = call(
        assemble_kernel, "assemble", "aaaa h", (f32(CELL, VEL),), (pltpu.SemaphoreType.DMA((4,)),)
    )(sc, *blocks)
    (table,) = call(table_kernel, "table", "vvvvv o", (f32(14, CELL),))(sc, *totals, cen)
    return dist_new, table


def solution(mesh):
    cells, vels = ("y", "core"), ("z", "x")
    placed = (
        P(cells, vels),
        P(cells),
        P(None, cells),
        P(None, None, cells),
        P(None, cells),
        P(cells, None),
        P(),
    )
    return jax.shard_map(
        local,
        mesh=jax.sharding.Mesh(mesh.devices.reshape(8, 4, 4, 2), ("z", "x", "y", "core")),
        in_specs=placed,
        out_specs=(P(cells, vels), P(None, cells)),
        check_vma=False,
    )
```

```python
import functools
import math

import jax
import jax.numpy as jnp
from jax import lax
from jax.experimental import pallas as pl
from jax.experimental.pallas import tpu as pltpu
from jax.sharding import PartitionSpec as P

VGRID = 64
SPEED_LIMIT = 10.0
TIME_STEP = 0.5
MU_REF = 0.5
VISC_EXPONENT = 0.81
DIFFUSIVITY_RAT = 2.0 / 3.0
INFLOW_SPEED = 5.0
H = 2.0 * SPEED_LIMIT / VGRID
WEIGHT = H**3 / (2.0 * math.pi) ** 1.5

CELL = 32
FACES = 4
LANES = 128
CHUNK = 2048
VEL = 8192
NB = 32
NC = 64
NVEL = 32
PIECES = 4
PAY = CHUNK + LANES
NSRC = 4 * NVEL
VMEM_LIMIT = 12 * 1024 * 1024
SMALL_LIMIT = 4 * 1024 * 1024

R_AREA, R_NORM, R_VOL, R_NEIGH, R_UNION, R_PAR = 0, 4, 16, 17, 21, 24


def place(level):
    return (level.astype(jnp.float32) + 0.5) * H - SPEED_LIMIT


def lane_iota(shape):
    return lax.broadcasted_iota(jnp.int32, shape, 1)


def row_iota(shape):
    return lax.broadcasted_iota(jnp.int32, shape, 0)


def rows_sum(x):
    return jnp.sum(x, axis=0, keepdims=True)


def pack(part, block):
    lane = lane_iota((4, LANES)) // CELL
    out = jnp.zeros((4, LANES), jnp.float32)
    for g in range(4):
        shift = CELL * ((g - block) % 4)
        rows = part[4 * g : 4 * g + 4]
        out = jnp.where(lane == g, pltpu.roll(rows, shift, 1) if shift else rows, out)
    return out


def first_kernel(sc, dist, area, normals, volume, neighbor, union, *refs):
    outs, packed, (d_ref, par_ref, sems), small = refs[0:4], refs[4], refs[5:8], refs[8:13]
    pairs = list(zip((area, normals, volume, neighbor, union), small))
    params = [pltpu.make_async_copy(a, b, sems.at[4 + i]) for i, (a, b) in enumerate(pairs)]
    for copy in params:
        copy.start()
    copies = []
    for group in range(4):
        rows = pl.ds(8 * group, 8)
        copies.append(pltpu.make_async_copy(dist.at[rows], d_ref.at[rows], sems.at[group]))
        copies[-1].start()
    y = sc[0]
    vel = sc[2]
    par_ref[...] = jnp.zeros((R_PAR, LANES), jnp.float32)
    for copy in params:
        copy.wait()
    area, normals, volume, neighbor, union = small
    par_ref[R_AREA : R_AREA + FACES, 0:CELL] = area[...]
    for d in range(3):
        par_ref[R_NORM + FACES * d : R_NORM + FACES * (d + 1), 0:CELL] = normals[d]
    par_ref[R_VOL : R_VOL + 1, 0:CELL] = volume[...]
    par_ref[R_NEIGH : R_NEIGH + FACES, 0:CELL] = neighbor[...].astype(jnp.float32)
    par_ref[R_UNION : R_UNION + 1, 0:16] = union[...].astype(jnp.float32)
    par = pltpu.roll(par_ref[...], y * CELL, 1)
    for out in outs:
        out[0:R_PAR, CHUNK:PAY] = par
        out[R_PAR:CELL, CHUNK:PAY] = jnp.zeros((CELL - R_PAR, LANES), jnp.float32)
    lane = lane_iota((8, LANES))
    par_y = (lane // NC).astype(jnp.float32) * H
    vz = place(lane % NC)
    base_y = par_y + (0.5 * H - SPEED_LIMIT)
    vx = [place(jnp.full((8, LANES), 2 * vel + a, jnp.int32)) for a in range(2)]
    wait_all(copies)
    centers = []
    for group in range(4):
        rows = slice(8 * group, 8 * group + 8)
        a0 = [None, None]
        a1 = None
        for a in range(2):
            for t in range(32):
                x = d_ref[rows, pl.ds((a * 32 + t) * LANES, LANES)]
                a0[a] = x if t == 0 else a0[a] + x
                if t:
                    a1 = x * float(t) if a1 is None else a1 + x * float(t)
        both = a0[0] + a0[1]
        totals = [both, a0[0] * vx[0] + a0[1] * vx[1], a1 * (2.0 * H) + both * base_y, both * vz]
        rho, *first = [jnp.sum(total, axis=1, keepdims=True) for total in totals]
        inv = 1.0 / jnp.maximum(rho, 1e-30)
        centers.append([jnp.clip(total * inv, -SPEED_LIMIT, SPEED_LIMIT) for total in first])
    tiles = []
    for group in range(4):
        rows = slice(8 * group, 8 * group + 8)
        cen_x, cen_y, cen_z = centers[group]
        cz = vz - cen_z
        cz2 = cz * cz
        start_y = base_y - cen_y
        sums = [None] * 13

        def add(index, value):
            sums[index] = value if sums[index] is None else sums[index] + value

        for a in range(2):
            p = [None] * 4
            for t in range(32):
                x = d_ref[rows, pl.ds((a * 32 + t) * LANES, LANES)]
                cy = start_y + 2.0 * H * t
                for power in range(4):
                    p[power] = x if t == 0 else p[power] + x
                    if power < 3:
                        x = x * cy
            cx = vx[a] - cen_x
            cx2 = cx * cx
            xz0 = (cx2 + cz2) * p[0] + p[2]
            add(0, p[0])
            add(1, cx * p[0])
            add(2, p[1])
            add(3, cz * p[0])
            add(4, cx2 * p[0])
            add(5, p[2])
            add(6, cz2 * p[0])
            add(7, cx * p[1])
            add(8, cx * cz * p[0])
            add(9, cz * p[1])
            add(10, cx * xz0)
            add(11, (cx2 + cz2) * p[1] + p[3])
            add(12, cz * xz0)
        cols = [jnp.sum(s, axis=1, keepdims=True) * WEIGHT for s in sums]
        cols += [cen_x, cen_y, cen_z]
        tile = jnp.zeros((8, LANES), jnp.float32)
        for q, col in enumerate(cols):
            tile = jnp.where(lane == q, col, tile)
        tiles.append(tile)
    for k, out in enumerate(outs):
        chunk = pl.multiple_of((y ^ k) * CHUNK, LANES)
        out[:, 0:CHUNK] = d_ref[:, pl.ds(chunk, CHUNK)]
    square = jnp.concatenate(tiles + [jnp.zeros((LANES - CELL, LANES), jnp.float32)], 0)
    block = pack(square.T[0:16], 0)
    for n in range(NSRC):
        packed[n] = block


def face_tables(par, vz):
    scaled = []
    for j in range(FACES):
        area = par[R_AREA + j : R_AREA + j + 1]
        n = [par[R_NORM + 4 * d + j : R_NORM + 4 * d + j + 1] * area for d in range(3)]
        scaled.append(n)
    return scaled


def start_all(pairs, sems):
    copies = [pltpu.make_async_copy(a, b, sems.at[i]) for i, (a, b) in enumerate(pairs)]
    for copy in copies:
        copy.start()
    return copies


def wait_all(copies):
    for copy in copies:
        copy.wait()


def to_lanes(stack, out):
    for blk in range(CHUNK // LANES):
        cols = slice(blk * LANES, (blk + 1) * LANES)
        out[cols, :] = stack[:, cols].T


def params_of(blocks):
    return functools.reduce(jnp.add, [blocks[n * CELL : n * CELL + R_PAR, CHUNK : CHUNK + LANES] for n in range(4)])


def prepare_kernel(sc, p0, p1, p2, p3, q0, q1, q2, q3, ui_ref, base, out_ref, num_ref, hot, par_ref, *scratch):
    pays, peers, dt_ref, gt_ref, ztab, ftab, sems, base_ref, hot_ref = scratch
    y, plane, first_b = sc[0], sc[3], sc[4]
    pairs = []
    for stack, blocks in ((pays, (p0, p1, p2, p3)), (peers, (q0, q1, q2, q3))):
        for k, block in enumerate(blocks):
            row = pl.multiple_of((y ^ k) * CELL, 8)
            pairs.append((block, stack.at[pl.ds(row, CELL)]))
    wait_all(start_all(pairs, sems))
    par = params_of(pays)
    par_ref[...] = par
    to_lanes(pays, dt_ref)
    to_lanes(peers, gt_ref)
    gather_table(sc, par, params_of(peers)[R_UNION : R_UNION + 1], ui_ref, hot_ref)
    masks = [(par[R_NEIGH + j : R_NEIGH + j + 1] >= CELL + 64 - 0.5).astype(jnp.float32) for j in range(FACES)]
    vz = place(row_iota((NC, LANES)))
    scaled = face_tables(par, vz)
    for j in range(FACES):
        ztab[j] = scaled[j][2] * vz
    ftab[...] = jnp.exp(-0.5 * vz * vz)
    vx = place(jnp.full((1, LANES), plane, jnp.int32))
    stay = par[R_VOL : R_VOL + 1] / TIME_STEP

    def body(b, _):
        vy = place(jnp.full((1, LANES), first_b + b, jnp.int32))
        free = jnp.exp(-0.5 * ((vx - INFLOW_SPEED) ** 2 + vy * vy))
        xy = [scaled[j][0] * vx + scaled[j][1] * vy for j in range(FACES)]
        for ct in range(NC // 8):
            rows = pl.ds(pl.multiple_of(b * NC + ct * 8, 8), 8)
            outflow = jnp.zeros((8, LANES), jnp.float32)
            inflow = jnp.zeros((8, LANES), jnp.float32)
            for j in range(FACES):
                s = xy[j] + ztab[j, ct * 8 : ct * 8 + 8]
                outflow = outflow + jnp.maximum(s, 0.0)
                inflow = inflow + jnp.maximum(-s, 0.0) * masks[j]
            out_ref[rows, :] = outflow
            base_ref[rows, :] = stay * dt_ref[rows, :] + (free * ftab[ct * 8 : ct * 8 + 8]) * inflow
        return 0

    lax.fori_loop(0, NB, body, 0)
    sends = start_all(((base_ref, base), (hot_ref, hot)), sems)
    faces(sc, dt_ref, gt_ref, base_ref, hot_ref, par_ref, num_ref, ztab)
    wait_all(sends)


def gather_table(sc, par, peer, ui_ref, hot_ref):
    core = sc[1]
    lane = lane_iota((1, LANES))
    own_rows = jnp.broadcast_to(par[R_UNION : R_UNION + 1], (LANES, LANES)).T
    peer_rows = jnp.broadcast_to(peer, (LANES, LANES)).T
    slots = row_iota((64, LANES))
    entries = row_iota((LANES, LANES))
    for j in range(FACES):
        e = par[R_NEIGH + j : R_NEIGH + j + 1].astype(jnp.int32)
        off = jnp.clip(e - CELL, 0, 63)
        source = off // 8
        position = rows_sum(jnp.where(slots == off, ui_ref[...], 0))
        entry = (source // 2) * CELL + position
        mine = (source % 2) == core
        found = jnp.where(entries == entry, jnp.where(mine, own_rows, peer_rows), 0.0)
        remote = rows_sum(found).astype(jnp.int32) + (source // 2) * CELL + jnp.where(mine, 0, LANES)
        local_row = (lane // CELL) * CELL + e
        target = jnp.where(e < CELL, local_row, jnp.where(e < CELL + 64, remote, -1))
        hot = (row_iota((2 * LANES, LANES)) == target).astype(jnp.float32)
        hot_ref[:, j * LANES : (j + 1) * LANES] = hot.astype(jnp.bfloat16)


def faces_kernel(sc, f, g, base, hot, par_ref, num_ref, ztab, f_ref, g_ref, base_ref, hot_ref, sems):
    wait_all(start_all(((f, f_ref), (g, g_ref), (base, base_ref), (hot, hot_ref)), sems))
    faces(sc, f_ref, g_ref, base_ref, hot_ref, par_ref, num_ref, ztab)


def faces(sc, f_ref, g_ref, base_ref, hot_ref, par_ref, num_ref, ztab):
    plane, first_b = sc[3], sc[4]
    par = par_ref[...]
    vz = place(row_iota((NC, LANES)))
    scaled = face_tables(par, vz)
    for j in range(FACES):
        ztab[j] = scaled[j][2] * vz
    vx = place(jnp.full((1, LANES), plane, jnp.int32))
    step_b = 8
    size = step_b * NC
    hot = jnp.concatenate([hot_ref[...]] * 2, 0)

    def body(it, _):
        rows = pl.ds(pl.multiple_of(it * size, size), size)
        x = jnp.concatenate([f_ref[rows, :], g_ref[rows, :]], 1)
        high = x.astype(jnp.bfloat16)
        low = (x - high.astype(jnp.float32)).astype(jnp.bfloat16)
        got = jnp.dot(jnp.concatenate([high, low], 1), hot, preferred_element_type=jnp.float32)
        for bb in range(step_b):
            vy = place(jnp.full((1, LANES), first_b + it * step_b + bb, jnp.int32))
            total = base_ref[pl.ds(pl.multiple_of(it * size + bb * NC, NC), NC), :]
            for j in range(FACES):
                xy = scaled[j][0] * vx + scaled[j][1] * vy
                s = xy + ztab[j]
                total = total - jnp.minimum(s, 0.0) * got[bb * NC : (bb + 1) * NC, j * LANES : (j + 1) * LANES]
            num_ref[pl.ds(pl.multiple_of(it * size + bb * NC, NC), NC), :] = total
        return 0

    lax.fori_loop(0, NB // step_b, body, 0)


def finish_rows(rho, center, s):
    sh = [s[i] / rho for i in (1, 2, 3)]
    mean = [center[i] + sh[i] for i in range(3)]
    xx, yy, zz, xy, xz, yz = s[4:10]
    trace = xx + yy + zz
    norm = sh[0] * sh[0] + sh[1] * sh[1] + sh[2] * sh[2]
    temp = (trace - rho * norm) / (3.0 * rho)
    proj = [
        xx * sh[0] + xy * sh[1] + xz * sh[2],
        xy * sh[0] + yy * sh[1] + yz * sh[2],
        xz * sh[0] + yz * sh[1] + zz * sh[2],
    ]
    heat = [0.5 * (s[10 + i] - 2.0 * proj[i] - sh[i] * trace + 2.0 * rho * norm * sh[i]) for i in range(3)]
    stress = [
        xx - rho * sh[0] * sh[0],
        yy - rho * sh[1] * sh[1],
        zz - rho * sh[2] * sh[2],
        xy - rho * sh[0] * sh[1],
        xz - rho * sh[0] * sh[2],
        yz - rho * sh[1] * sh[2],
    ]
    return [rho] + mean + [temp] + stress + heat


def moments_first(part_ref):
    every = part_ref[...].reshape(NVEL, 4, 4, LANES)
    lane = lane_iota((NVEL, LANES)) // CELL
    q = [None] * 16
    for r in range(4):
        blocks = [every[:, b, r, :] for b in range(4)]
        for g in range(4):
            row = jnp.zeros((NVEL, LANES), jnp.float32)
            for b in range(4):
                shift = CELL * ((b - g) % 4)
                row = jnp.where(lane == b, pltpu.roll(blocks[b], shift, 1) if shift else blocks[b], row)
            q[4 * g + r] = row
    rho_d, m, s, heat, cen = q[0], q[1:4], q[4:10], q[10:13], q[13:16]
    rho = rows_sum(rho_d)
    u = [rows_sum(m[i] + rho_d * cen[i]) / rho for i in range(3)]
    d = [cen[i] - u[i] for i in range(3)]
    tensor = ((0, 3, 4), (3, 1, 5), (4, 5, 2))
    pairs = ((0, 0), (1, 1), (2, 2), (0, 1), (0, 2), (1, 2))
    d2 = d[0] * d[0] + d[1] * d[1] + d[2] * d[2]
    m_d = m[0] * d[0] + m[1] * d[1] + m[2] * d[2]
    total = s[0] + s[1] + s[2] + 2.0 * m_d + rho_d * d2
    sums = [rho] + [rows_sum(m[i] + rho_d * d[i]) for i in range(3)]
    for n, (i, j) in enumerate(pairs):
        sums.append(rows_sum(s[n] + m[i] * d[j] + d[i] * m[j] + rho_d * d[i] * d[j]))
    for i in range(3):
        along = s[tensor[i][0]] * d[0] + s[tensor[i][1]] * d[1] + s[tensor[i][2]] * d[2]
        sums.append(rows_sum(heat[i] + 2.0 * along + m[i] * d2 + d[i] * total))
    return finish_rows(rho, u, sums)


def moments_next(part_ref, cen_ref):
    total = part_ref[0]
    for n in range(1, NVEL):
        total = total + part_ref[n]
    s = [total[i : i + 1] for i in range(13)]
    return finish_rows(s[0], [cen_ref[i : i + 1] for i in range(3)], s)


def relax(sc, moments, num_ref, out_ref, par_ref, f_out, part_ref, cen_ref, tabs):
    zt_ref, zq_ref, zg_ref, cz_ref, f_ref, sems = tabs
    size = CHUNK // PIECES
    moments = moments()
    plane, first_b = sc[3], sc[4]
    rho, ux, uy, uz, temp = moments[0:5]
    heat = moments[11:14]
    vol = par_ref[R_VOL : R_VOL + 1]
    log_t = jnp.log(temp)
    rate = rho * jnp.exp((1.0 - VISC_EXPONENT) * log_t) * (1.0 / MU_REF)
    volrate = vol * rate
    fixed = vol / TIME_STEP + volrate
    scale = volrate * rho * jnp.exp(-1.5 * log_t)
    inv_t = 1.0 / temp
    mult = (1.0 - DIFFUSIVITY_RAT) / (5.0 * rho * temp * temp)
    heat = [mult * h for h in heat]
    cx = place(jnp.full((1, LANES), plane, jnp.int32)) - ux
    cx2 = cx * cx
    cz = place(row_iota((NC, LANES))) - uz
    cz_ref[...] = cz
    zt = cz * cz * inv_t
    zt_ref[...] = zt
    zg_ref[...] = jnp.exp(-0.5 * zt)
    zq_ref[...] = cz * heat[2]
    x_t = cx2 * inv_t
    x_q = cx * heat[0]
    zero = jnp.zeros((8, LANES), jnp.float32)

    unroll = 4

    def body(step, acc):
        acc = list(acc)
        for part in range(unroll):
            b = step * unroll + part
            cy = place(jnp.full((1, LANES), first_b + b, jnp.int32)) - uy
            cy2 = cy * cy
            xy_t = x_t + cy2 * inv_t
            xy_g = scale * jnp.exp(-0.5 * xy_t)
            xy_t = xy_t - 5.0
            xy_q = x_q + cy * heat[1]
            p = [None] * 4
            for ct in range(NC // 8):
                loc = slice(ct * 8, ct * 8 + 8)
                rows = pl.ds(pl.multiple_of(b * NC + ct * 8, 8), 8)
                poly = 1.0 + (xy_q + zq_ref[loc]) * (xy_t + zt_ref[loc])
                num = num_ref[rows, :] + (xy_g * zg_ref[loc]) * poly
                den = fixed + out_ref[rows, :]
                f = num / den
                f_ref[rows, :] = f
                c = cz_ref[loc]
                for power in range(4):
                    p[power] = f if p[power] is None else p[power] + f
                    if power < 3:
                        f = f * c
            new = [
                p[0], cy * p[0], cy2 * p[0], cy2 * cy * p[0],
                p[1], cy * p[1], cy2 * p[1],
                p[2], cy * p[2],
                p[3],
            ]
            acc = [o + n for o, n in zip(acc, new)]
        return tuple(acc)

    acc = (zero,) * 10
    sends = []
    steps = NB // unroll // PIECES
    for piece in range(PIECES):
        acc = lax.fori_loop(piece * steps, (piece + 1) * steps, body, acc)
        if f_out is not None:
            rows = pl.ds(piece * size, size)
            sends += start_all([(f_ref.at[rows], f_out.at[rows])], sems.at[pl.ds(piece, 1)])
    t0, t0y, t0yy, t0yyy, t1, t1y, t1yy, t2, t2y, t3 = [rows_sum(a) * WEIGHT for a in acc]
    rows = [
        t0, cx * t0, t0y, t1,
        cx2 * t0, t0yy, t2, cx * t0y, cx * t1, t1y,
        cx * (cx2 * t0 + t0yy + t2),
        cx2 * t0y + t0yyy + t2y,
        cx2 * t1 + t1yy + t3,
    ]
    for i, row in enumerate(rows):
        part_ref[i : i + 1] = row
    part_ref[13:16] = jnp.zeros((3, LANES), jnp.float32)
    for i, row in enumerate((ux, uy, uz)):
        cen_ref[i : i + 1] = row
    cen_ref[3:8] = jnp.zeros((5, LANES), jnp.float32)
    wait_all(sends)


def relax_first_kernel(sc, parts, num, out, par_ref, f_out, part_ref, cen_ref, *tabs):
    relax(sc, lambda: moments_first(parts), num, out, par_ref, f_out, part_ref, cen_ref, tabs)


def relax_next_kernel(sc, parts, num, out, par_ref, old_ref, f_out, part_ref, cen_ref, *tabs):
    relax(sc, lambda: moments_next(parts, old_ref), num, out, par_ref, f_out, part_ref, cen_ref, tabs)


def relax_last_kernel(sc, parts, num, out, par_ref, old_ref, f_out, copies, cen_ref, *scratch):
    tabs, part_ref = scratch[0:6], scratch[6]
    relax(sc, lambda: moments_next(parts, old_ref), num, out, par_ref, f_out, part_ref, cen_ref, tabs)
    part = part_ref[...]
    for n in range(NVEL):
        copies[n] = part


def blocks_kernel(sc, f_ref, o0, o1, o2, o3, stack):
    for blk in range(CHUNK // LANES):
        cols = slice(blk * LANES, (blk + 1) * LANES)
        stack[:, cols] = f_ref[cols, :].T
    for k, o in enumerate((o0, o1, o2, o3)):
        o[...] = stack[pl.ds(pl.multiple_of((sc[0] ^ k) * CELL, 8), CELL), :]


def sum_kernel(p0, p1, p2, p3, out):
    total = (p0[...] + p1[...]) + (p2[...] + p3[...])
    for n in range(NVEL):
        out[n] = total


def total_kernel(sc, parts, p0, p1, p2, p3):
    total = functools.reduce(jnp.add, [parts[n] for n in range(NVEL)])
    total = pltpu.roll(total, (LANES - sc[0] * CELL) % LANES, 1)
    y = sc[0]
    for k, out in enumerate((p0, p1, p2, p3)):
        out[...] = pack(pltpu.roll(total, (4 + y - (y ^ k)) % 4 * CELL, 1), 0)


def assemble_kernel(sc, r0, r1, r2, r3, out, sems):
    pairs = []
    for k, r in enumerate((r0, r1, r2, r3)):
        pairs.append((r, out.at[:, pl.ds(pl.multiple_of((sc[0] ^ k) * CHUNK, LANES), CHUNK)]))
    wait_all(start_all(pairs, sems))


def table_kernel(sc, t0, t1, t2, t3, cen_ref, table_ref):
    total = (t0[...] + t1[...]) + (t2[...] + t3[...])
    cen = pltpu.roll(cen_ref[...], (LANES - sc[0] * CELL) % LANES, 1)
    sums = [None] * 16
    for g in range(4):
        rows = pltpu.roll(total, LANES - CELL * g, 1) if g else total
        for r in range(4):
            sums[4 * g + r] = rows[r : r + 1]
    rows = finish_rows(sums[0], [cen[i : i + 1] for i in range(3)], sums)
    for i, row in enumerate(rows):
        table_ref[i : i + 1] = row[:, 0:CELL]


def call(kernel, name, spaces, out_shapes, scratch=(), scalars=True, limit=VMEM_LIMIT):
    spec = {"v": pl.BlockSpec(memory_space=pltpu.VMEM)}
    spec["o"] = spec["v"]
    spec["a"] = spec["h"] = pl.BlockSpec(memory_space=pl.ANY)
    spaces, out_spaces = spaces.split()
    place_out = {"v": pltpu.VMEM, "h": pltpu.HBM, "o": jax.ShapeDtypeStruct}
    shapes = tuple(place_out[space](o.shape, o.dtype) for space, o in zip(out_spaces, out_shapes))
    specs = tuple(spec[space] for space in out_spaces)
    kernel_call = pl.pallas_call(
        kernel,
        name=name,
        out_shape=shapes,
        in_specs=[pl.BlockSpec(memory_space=pltpu.SMEM)] * scalars + [spec[space] for space in spaces],
        out_specs=specs,
        scratch_shapes=list(scratch),
        compiler_params=pltpu.CompilerParams(vmem_limit_bytes=limit),
        cost_estimate=pl.CostEstimate(flops=1000, bytes_accessed=1000, transcendentals=0),
    )

    def run(*args):
        first = len(args) - len(spaces)
        placed = [
            pltpu.with_memory_space_constraint(x, pltpu.HBM) if space == "h" else x
            for space, x in zip(spaces, args[first:])
        ]
        return kernel_call(*args[:first], *placed)

    return run


def f32(*shape):
    return jax.ShapeDtypeStruct(shape, jnp.float32)


def toward_y(values):
    out = [values[0]]
    for k in (1, 3, 2):
        out.append(lax.ppermute(values[k], "y", [(m, m ^ k) for m in range(4)]))
    return [out[0], out[1], out[3], out[2]]


def other_core(value):
    return lax.ppermute(value, "core", [(0, 1), (1, 0)])


def spread(copies):
    return lax.all_to_all(copies, ("z", "x"), 0, 0)


def exchange(packed):
    return lax.all_to_all(packed, ("z", "x", "y"), 0, 0)


def summed(part, f):
    copies = call(sum_kernel, "copies", "vvvv v", (f32(NVEL, 16, LANES),), scalars=False, limit=SMALL_LIMIT)
    g = other_core(f)
    arrived = toward_y([part] * 4)
    return spread(copies(*arrived)[0]), g


def local(dist_old, volume, area, normals, neighbor, union_rows, union_index):
    vel = lax.axis_index("z") * 4 + lax.axis_index("x")
    y, core = lax.axis_index("y"), lax.axis_index("core")
    sc = jnp.stack([y, core, vel, 2 * vel + y // 2, NB * (y % 2)]).astype(jnp.int32)
    mine = lax.dynamic_index_in_dim(union_index.reshape(8, 4, 2, 8), core, 2, keepdims=False)
    slots = jnp.repeat(jnp.transpose(mine, (0, 2, 1)).reshape(64, 4), CELL, axis=1)

    *pays, packed = call(
        first_kernel,
        "first",
        "hhhhhh vvvvo",
        (f32(CELL, PAY),) * 4 + (f32(NSRC, 4, LANES),),
        (
            pltpu.VMEM((CELL, VEL), jnp.float32),
            pltpu.VMEM((R_PAR, LANES), jnp.float32),
            pltpu.SemaphoreType.DMA((9,)),
            pltpu.VMEM((FACES, CELL), jnp.float32),
            pltpu.VMEM((3, FACES, CELL), jnp.float32),
            pltpu.VMEM((1, CELL), jnp.float32),
            pltpu.VMEM((FACES, CELL), jnp.int32),
            pltpu.VMEM((1, 16), jnp.int32),
        ),
    )(sc, dist_old, area, normals, volume[None], neighbor, union_rows)
    got = toward_y(pays)
    peers = [other_core(g) for g in got]
    parts = exchange(packed)
    state = f32(CHUNK, LANES)
    big = pltpu.VMEM((CHUNK, LANES), jnp.float32)
    hots = pltpu.VMEM((2 * LANES, FACES * LANES), jnp.bfloat16)
    ztab = (pltpu.VMEM((FACES, NC, LANES), jnp.float32),)
    base, outflow, num, hot, par = call(
        prepare_kernel,
        "prepare",
        "ahhhhhhhv hvvhv",
        (state, state, state, jax.ShapeDtypeStruct((2 * LANES, FACES * LANES), jnp.bfloat16), f32(R_PAR, LANES)),
        (
            pltpu.VMEM((LANES, PAY), jnp.float32),
            pltpu.VMEM((LANES, PAY), jnp.float32),
            big,
            big,
        )
        + ztab
        + (pltpu.VMEM((NC, LANES), jnp.float32), pltpu.SemaphoreType.DMA((8,)), big, hots),
    )(sc, *got, *peers, slots)
    tabs = (pltpu.VMEM((NC, LANES), jnp.float32),) * 4 + (big, pltpu.SemaphoreType.DMA((PIECES,)))
    faces_next = call(
        faces_kernel, "faces", "aahhv v", (state,), ztab + (big, big, big, hots, pltpu.SemaphoreType.DMA((4,)))
    )
    small = (f32(16, LANES), f32(8, LANES))

    f, part, cen = call(relax_first_kernel, "relax_first", "vvvv vvv", (state,) + small, tabs)(
        sc, parts, num, outflow, par
    )
    relax_next = call(relax_next_kernel, "relax_next", "vvvvv vvv", (state,) + small, tabs)
    parts, g = summed(part, f)
    (num,) = faces_next(sc, f, g, base, hot, par)
    f, part, cen = relax_next(sc, parts, num, outflow, par, cen)
    parts, g = summed(part, f)
    (num,) = faces_next(sc, f, g, base, hot, par)
    f, copies, cen = call(
        relax_last_kernel,
        "relax_last",
        "vvvvv vov",
        (state, f32(NVEL, 16, LANES), f32(8, LANES)),
        tabs + (pltpu.VMEM((16, LANES), jnp.float32),),
    )(sc, parts, num, outflow, par, cen)
    chunks = call(
        blocks_kernel,
        "blocks",
        "v vvvv",
        (f32(CELL, CHUNK),) * 4,
        (pltpu.VMEM((LANES, CHUNK), jnp.float32),),
    )(sc, f)
    parts = spread(copies)
    blocks = toward_y(chunks)
    packs = call(total_kernel, "total", "v vvvv", (f32(4, LANES),) * 4, limit=SMALL_LIMIT)(sc, parts)
    totals = toward_y(packs)
    (dist_new,) = call(
        assemble_kernel, "assemble", "aaaa h", (f32(CELL, VEL),), (pltpu.SemaphoreType.DMA((4,)),)
    )(sc, *blocks)
    (table,) = call(table_kernel, "table", "vvvvv o", (f32(14, CELL),))(sc, *totals, cen)
    return dist_new, table


def solution(mesh):
    cells, vels = ("y", "core"), ("z", "x")
    placed = (
        P(cells, vels),
        P(cells),
        P(None, cells),
        P(None, None, cells),
        P(None, cells),
        P(cells, None),
        P(),
    )
    return jax.shard_map(
        local,
        mesh=jax.sharding.Mesh(mesh.devices.reshape(8, 4, 4, 2), ("z", "x", "y", "core")),
        in_specs=placed,
        out_specs=(P(cells, vels), P(None, cells)),
        check_vma=False,
    )
```
